32 devices in a mesh: groups: 2 (over y), dp: 4 (over z), mp: 4 (over x, core).
Axes of the slice: x: 2, y: 2, z: 4, core: 2. Of those that a mesh axis runs over, the one named last changes fastest.
Arguments:
- qkv_home: bfloat16 [8, 764, 3, 3072], P(('groups', 'dp'), None, None, 'mp'), parts along dimension 0, may hold values from -6 to 6
- resid_home: bfloat16 [8, 764, 6144], P(('groups', 'dp'), None, 'mp'), parts along dimension 0, may hold values from -6 to 6
- out_weight: bfloat16 [3072, 6144], P('dp', 'mp'), may hold values from -0.109375 to 0.109375
- label_weight: bfloat16 [6144, 12288], P('mp', 'dp'), may hold values from -0.21875 to 0.21875
- label_bias: float32 [12288], P('dp'), may hold values from -5 to 5
- query_gain: float32 [128], replicated, may hold values from 0.25 to 1.75
- key_gain: float32 [128], replicated, may hold values from 0.25 to 1.75
- patch_counts: int32 [8, 4], P('groups'), parts along dimension 0, may hold values from 1 to 191, as said below
- move_plan: int32 [8, 4], P('groups'), parts along dimension 0, may hold values from 0 to 3, as said below
- segment_ids: int32 [8, 764], P(('groups', 'dp')), parts along dimension 0, may hold values from 0 to 4, as said below
Outputs:
- mixed: bfloat16 [8, 384, 6144], P(('groups', 'dp'), None, 'mp'), parts along dimension 0
- labels: float32 [8, 4, 12288], P(('groups', 'dp'), 'mp'), parts along dimension 0
The draws below stay inside these ranges and needn't reach their ends.
There are 2 independent parts, one for each index of `groups`. The reference program is written for one: setup_inputs(seed, part) draws one part's arguments, and reference() takes and returns one part's arrays. A program takes and returns all parts, laid end to end along the dimension named above; an argument that names none is the same for every part. Nothing has to cross between parts.
Inputs may be any that keep to these rules, and one draw needn't show every extreme that they name: `patch_counts`: home row r holds its 4 images packed in the order j; every destination row receives exactly one image from every home row, 384 patches in all; every draw holds an image of 191 patches. Every row of move_plan is a permutation, and every destination row appears once in every column, so each destination receives one image from each home row. `segment_ids`: image j of home row r has id j on its patch_counts[r, j] slots, which follow those of image j - 1; slots after the last image have id 4.
All inputs are finite; a program needn't handle non-finite values.
Results may differ from the reference program's by a relative error of at most 0.0065.
Values may be sent and summed in bfloat16 or wider, within the bound.
No kernel may reach another device: no remote copies, remote signals or barrier semaphores. Data moves between devices by JAX's collectives and lax.ppermute only.
A program may use at most 64 MiB of HBM per device.

```python
import math
import jax
import jax.numpy as jnp
from jax import lax

D = 6144
HD = 128
HEADS = 24
CLASSES = 12288
TOK = 384
ROWS = 4
MEAN = 96
HOME = 764


def draw_layout(key):
    base_key = jax.random.fold_in(key, 7)
    sub_keys = jax.random.split(base_key, 6)
    row_ids = jnp.arange(ROWS, dtype=jnp.int32)
    col_shift = jax.random.permutation(sub_keys[0], ROWS).astype(jnp.int32)
    row_shift = jax.random.permutation(sub_keys[1], ROWS).astype(jnp.int32)
    move_plan = (col_shift[None, :] + row_shift[:, None]) % ROWS
    pairing = jax.random.permutation(sub_keys[2], ROWS).astype(jnp.int32)
    centers = jax.random.randint(sub_keys[3], (ROWS // 2, 1), 1, 2 * MEAN)
    jitter = jax.random.randint(sub_keys[4], (ROWS // 2, ROWS), -(MEAN // 2), MEAN // 2 + 1)
    heavy = jnp.clip(centers + jitter, 1, 2 * MEAN - 1)
    full_dest = jax.random.randint(sub_keys[5], (ROWS // 2, 1), 0, ROWS)
    heavy = jnp.where(row_ids[None, :] == full_dest, 2 * MEAN - 1, heavy).astype(jnp.int32)
    loads = jnp.zeros((ROWS, ROWS), jnp.int32)
    loads = loads.at[pairing[0::2]].set(heavy)
    loads = loads.at[pairing[1::2]].set(2 * MEAN - heavy)
    counts = jnp.take_along_axis(loads, move_plan, axis=1)
    image_ends = jnp.cumsum(counts, axis=1)
    slot_ids = jnp.arange(HOME, dtype=jnp.int32)
    segments = jnp.sum((slot_ids[None, :, None] >= image_ends[:, None, :]).astype(jnp.int32), axis=2)
    return (counts.astype(jnp.int32), move_plan.astype(jnp.int32), segments.astype(jnp.int32))


def draw_patch_counts(key, part):
    return draw_layout(key)[0]


def draw_move_plan(key, part):
    return draw_layout(key)[1]


def draw_segment_ids(key, part):
    return draw_layout(key)[2]


def steps_of(own_key, dims, cuts, low, largest):
    factor_of, own = 1.0, jax.random.fold_in(own_key, 6)
    for axis_at, parts in cuts:
        heights = jnp.exp(jax.random.uniform(jax.random.fold_in(own, axis_at), (parts,), jnp.float32, low / len(cuts), largest / len(cuts)))
        factor_of = factor_of * jnp.repeat(heights, dims[axis_at] // parts).reshape([-1 if axis == axis_at else 1 for axis in range(len(dims))])
    return factor_of


def centred(rng, shape, width, bound, cuts=(), held_as=jnp.bfloat16):
    factor_of = steps_of(rng, shape, cuts, -0.22, 0.18) if cuts else 1.0
    result = jax.random.normal(rng, shape, jnp.float32) * width * factor_of
    return jnp.minimum(jnp.maximum(result, -bound), bound).astype(held_as)


def setup_inputs(seed: int = 0, part: int = 0) -> dict:
    key_of = jax.random.split(jax.random.key(seed), 11)
    part_keys = jax.random.split(jax.random.fold_in(key_of[10], part), 11)
    return {
        "qkv_home": centred(part_keys[0], (ROWS, HOME, 3, HEADS * HD), 1.0, 6.0, ((0, 4), (3, 4))),
        "resid_home": centred(part_keys[1], (ROWS, HOME, D), 1.0, 6.0, ((0, 4), (2, 4))),
        "out_weight": centred(key_of[2], (HEADS * HD, D), (HEADS * HD) ** -0.5, 0.109375, ((0, 4), (1, 4))),
        "label_weight": centred(key_of[3], (D, CLASSES), (D // 8) ** -0.5, 0.21875, ((0, 4), (1, 4))),
        "label_bias": centred(key_of[4], (CLASSES,), 1.0, 5.0, ((0, 4),), jnp.float32),
        "query_gain": jnp.clip(1.0 + 0.15 * jax.random.normal(key_of[5], (HD,), jnp.float32), 0.25, 1.75),
        "key_gain": jnp.clip(1.0 + 0.15 * jax.random.normal(key_of[6], (HD,), jnp.float32), 0.25, 1.75),
        "patch_counts": draw_patch_counts(jax.random.fold_in(jax.random.fold_in(key_of[10], part), 71), part),
        "move_plan": draw_move_plan(jax.random.fold_in(jax.random.fold_in(key_of[10], part), 71), part),
        "segment_ids": draw_segment_ids(jax.random.fold_in(jax.random.fold_in(key_of[10], part), 71), part),
    }


EPSILON = 1e-06

def head_norm(values, norm_gain):
    center = values - lax.optimization_barrier(jnp.mean(values, axis=-1, keepdims=True))
    spread = lax.optimization_barrier(jnp.mean(center * center, axis=-1, keepdims=True))
    return center * lax.rsqrt(spread + EPSILON) * norm_gain

def rounded(values):
    return lax.optimization_barrier(values.astype(jnp.bfloat16)).astype(jnp.float32)

def attend(qkv_rows, seg_rows, query_gain, key_gain):
    length = qkv_rows.shape[0]
    head_count = qkv_rows.shape[2] // HD
    split_parts = qkv_rows.astype(jnp.float32).reshape(length, 3, head_count, HD)
    queries = rounded(head_norm(split_parts[:, 0], query_gain))
    key_rows = rounded(head_norm(split_parts[:, 1], key_gain))
    scores = jnp.einsum('qhd,khd->hqk', queries, key_rows) / math.sqrt(HD)
    same_image = (seg_rows[:, None] == seg_rows[None, :]).astype(jnp.float32)
    raised = jnp.exp(scores) * same_image[None]
    weights = rounded(raised / lax.optimization_barrier(jnp.sum(raised, axis=-1, keepdims=True)))
    head_out = jnp.einsum('hqk,khd->qhd', weights, split_parts[:, 2])
    return head_out.reshape(length, head_count * HD).astype(jnp.bfloat16)

def reference(qkv_home, resid_home, out_weight, label_weight, label_bias, query_gain, key_gain, patch_counts, move_plan, segment_ids):
    row_count = patch_counts.shape[0]
    home_slots = qkv_home.shape[1]
    image_ids = jnp.arange(row_count, dtype=jnp.int32)

    def one_row(entry):
        qkv_rows, resid_rows, seg_rows, count_row = entry
        heads_done = attend(qkv_rows, seg_rows, query_gain, key_gain)
        projected = jnp.dot(heads_done, out_weight, preferred_element_type=jnp.float32)
        row_mixed = (resid_rows.astype(jnp.float32) + projected).astype(jnp.bfloat16)
        member = (image_ids[:, None] == seg_rows[None, :]).astype(jnp.bfloat16)
        image_sums = jnp.dot(member, row_mixed, preferred_element_type=jnp.float32)
        row_pooled = (image_sums / count_row[:, None].astype(jnp.float32)).astype(jnp.bfloat16)
        return (row_mixed, row_pooled)
    home_mixed, pooled = lax.map(one_row, (qkv_home, resid_home, segment_ids, patch_counts))
    logits = jnp.dot(pooled.reshape(row_count * row_count, -1), label_weight, preferred_element_type=jnp.float32)
    logits = logits + label_bias.astype(jnp.float32)[None, :]
    labels = jax.nn.sigmoid(logits).reshape(row_count, row_count, -1)
    image_ends = jnp.cumsum(patch_counts, axis=1)
    starts = image_ends - patch_counts
    matches = (move_plan[:, :, None] == image_ids[None, None, :]).astype(jnp.int32)
    image_sizes = lax.optimization_barrier(jnp.sum(patch_counts[:, :, None] * matches, axis=1))
    firsts = lax.optimization_barrier(jnp.sum(starts[:, :, None] * matches, axis=1))
    column_ends = jnp.cumsum(image_sizes, axis=0)
    column_starts = column_ends - image_sizes
    slot_ids = jnp.arange(TOK, dtype=jnp.int32)
    source = lax.optimization_barrier(jnp.sum((slot_ids[None, :, None] >= column_ends.T[:, None, :]).astype(jnp.int32), axis=2))
    chosen = (source[:, :, None] == image_ids[None, None, :]).astype(jnp.int32)
    shift_by = lax.optimization_barrier(jnp.sum(chosen * (firsts.T[:, None, :] - column_starts.T[:, None, :]), axis=2))
    flat_index = (source * home_slots + shift_by + slot_ids[None, :]).astype(jnp.int32)
    mixed = jnp.take(home_mixed.reshape(row_count * home_slots, -1), flat_index.reshape(-1), axis=0)
    mixed = mixed.reshape(row_count, TOK, -1)
    return (mixed, labels)
```

```python
import math

import jax
import jax.numpy as jnp
from jax import lax
from jax.experimental import pallas as pl
from jax.experimental.pallas import tpu as pltpu
from jax.sharding import PartitionSpec as P

TOK = 384
CHUNKS = 2
VMEM_BYTES = 48 * 1024 * 1024


EPSILON = 1e-06


def head_norm(values, norm_gain):
    center = values - jnp.mean(values, axis=-1, keepdims=True)
    spread = jnp.mean(center * center, axis=-1, keepdims=True)
    return center * lax.rsqrt(spread + EPSILON) * norm_gain


def shifted(count, by):
    return [(i, (i + by) % count) for i in range(count)]


def crossed(count, by):
    return [(i, i ^ by) for i in range(count)]


def dot32(left, right):
    return jnp.dot(left, right, preferred_element_type=jnp.float32)


def at(values, index, axis=0):
    return lax.dynamic_index_in_dim(values, index, axis, keepdims=False)


def image_for(counts_ref, plan_ref, row, dest, images):
    image, first, size, before = 0, 0, 0, 0
    for j in range(images):
        count = counts_ref[row, j]
        hit = plan_ref[row, j] == dest
        image = jnp.where(hit, j, image)
        first = jnp.where(hit, before, first)
        size = jnp.where(hit, count, size)
        before = before + count
    return image, first, size


def attend_kernel(
    rows,
    span,
    place_ref,
    counts_ref,
    plan_ref,
    qkv_ref,
    resid_ref,
    query_gain_ref,
    key_gain_ref,
    *rest,
):
    heads_ref, sent_ref, head_means_ref, resid_means_ref, means_ref = rest[-5:]
    k = pl.program_id(0)
    my_row = place_ref[0]
    image, first, size = image_for(
        counts_ref, plan_ref, my_row, lax.rem(my_row + k, rows), rows
    )
    window = span + 16
    begin = pl.multiple_of(first // 16 * 16, 16)
    shift = first - begin
    taken = lax.broadcasted_iota(jnp.int32, (span, window), 0)
    slot = lax.broadcasted_iota(jnp.int32, (span, window), 1)
    select = ((slot - taken == shift) & (taken < size)).astype(jnp.float32).astype(jnp.bfloat16)
    count = size.astype(jnp.float32)
    resid = dot32(select, resid_ref[pl.ds(begin, window), :])
    sent_ref[...] = resid.astype(jnp.bfloat16)
    here = lax.broadcasted_iota(jnp.int32, (rows, 1), 0) == image
    resid_mean = jnp.sum(resid, axis=0, keepdims=True) / count
    resid_means_ref[...] = jnp.where(here, resid_mean, resid_means_ref[...])
    queries = dot32(select, qkv_ref[0, pl.ds(begin, window), :])
    keys = dot32(select, qkv_ref[1, pl.ds(begin, window), :])
    values = dot32(select, qkv_ref[2, pl.ds(begin, window), :]).astype(jnp.bfloat16)
    head_width = query_gain_ref.shape[1]
    inside = lax.broadcasted_iota(jnp.int32, (span, span), 1) < size
    kept = lax.broadcasted_iota(jnp.int32, (span, 1), 0) < size
    for h in range(heads_ref.shape[1] // head_width):
        columns = slice(h * head_width, (h + 1) * head_width)
        query = head_norm(queries[:, columns], query_gain_ref[...]).astype(jnp.bfloat16)
        key = head_norm(keys[:, columns], key_gain_ref[...]).astype(jnp.bfloat16)
        scores = lax.dot_general(
            query, key, (((1,), (1,)), ((), ())), preferred_element_type=jnp.float32
        ) * (1.0 / math.sqrt(head_width))
        raised = jnp.where(inside, jnp.exp(scores), 0.0)
        scale = jnp.where(kept, 1.0 / jnp.sum(raised, axis=-1, keepdims=True), 0.0)
        weights = (raised * scale).astype(jnp.bfloat16)
        head = dot32(weights, values[:, columns]).astype(jnp.bfloat16)
        heads_ref[:, columns] = head
        head_mean = jnp.sum(head.astype(jnp.float32), axis=0, keepdims=True) / count
        means_ref[:, columns] = jnp.where(here, head_mean, means_ref[:, columns])

    @pl.when(k == rows - 1)
    def _():
        head_means_ref[...] = means_ref[...].astype(jnp.bfloat16)


def attend(place, counts, plan, qkv, resid, query_gain, key_gain, span, after):
    rows = counts.shape[0]
    local, features = qkv.shape[2], resid.shape[1]
    whole = pl.BlockSpec(memory_space=pltpu.VMEM)
    fixed = lambda shape: pl.BlockSpec(shape, lambda k, *_: (0,) * len(shape))
    return pl.pallas_call(
        lambda *refs: attend_kernel(rows, span, *refs),
        grid_spec=pltpu.PrefetchScalarGridSpec(
            num_scalar_prefetch=3,
            grid=(rows,),
            in_specs=[fixed(x.shape) for x in (qkv, resid, query_gain, key_gain)]
            + [pl.BlockSpec(memory_space=pl.ANY)] * len(after),
            out_specs=[
                pl.BlockSpec((span, local), lambda k, *_: (k, 0)),
                pl.BlockSpec((span, features), lambda k, *_: (k, 0)),
                fixed((rows, local)),
                fixed((rows, features)),
            ],
            scratch_shapes=[pltpu.VMEM((rows, local), jnp.float32)],
        ),
        out_shape=[
            jax.ShapeDtypeStruct((rows * span, local), jnp.bfloat16),
            jax.ShapeDtypeStruct((rows * span, features), jnp.bfloat16),
            jax.ShapeDtypeStruct((rows, local), jnp.bfloat16),
            jax.ShapeDtypeStruct((rows, features), jnp.float32),
        ],
        compiler_params=pltpu.CompilerParams(vmem_limit_bytes=VMEM_BYTES),
        cost_estimate=pl.CostEstimate(
            flops=10_000_000_000, bytes_accessed=12_000_000, transcendentals=1_000_000
        ),
        name="attend",
    )(place, counts, plan, qkv, resid, query_gain, key_gain, *after)


def project_kernel(rows, place_ref, *refs):
    head_refs = refs[:rows]
    own_ref = refs[rows]
    piece_refs = refs[rows + 1 : rows + 1 + 2 * (rows - 1)]
    resid_ref = refs[3 * rows - 1]
    out_refs = refs[3 * rows : 4 * rows]
    held_ref, sems = refs[4 * rows :]
    my_row, my_part, my_group = place_ref[0], place_ref[1], place_ref[2]
    half = held_ref.shape[2]

    @pl.when(pl.program_id(0) == 0)
    def _():
        copies = [
            pltpu.make_async_copy(
                head_refs[x].at[:, s * half : (s + 1) * half],
                held_ref.at[2 * (x ^ my_part) + s],
                sems.at[x, s],
            )
            for x in range(rows)
            for s in range(2)
        ]
        for copy in copies:
            copy.start()
        for copy in copies:
            copy.wait()

    total = resid_ref[...].astype(jnp.float32)
    for s in range(2):
        total = total + dot32(held_ref[2 * my_row + s], own_ref[s * half : (s + 1) * half, :])
    for step in range(1, rows):
        row = lax.rem(my_row - step + rows, rows)
        for which in range(2):
            piece_ref = piece_refs[2 * (step - 1) + which]
            total = total + dot32(held_ref[2 * row + (my_group ^ which)], piece_ref[...])
    span = out_refs[0].shape[0]
    for k in range(rows):
        out_refs[k][...] = total[k * span : (k + 1) * span].astype(jnp.bfloat16)


def project(place, heads, out_weight, pieces, resid, chunk, width, span):
    rows = len(heads)
    length, depth = heads[0].shape
    half = depth // 2
    tile = 256
    tiles = width // tile
    first = chunk * tiles
    return pl.pallas_call(
        lambda *refs: project_kernel(rows, *refs),
        grid_spec=pltpu.PrefetchScalarGridSpec(
            num_scalar_prefetch=1,
            grid=(tiles,),
            in_specs=[pl.BlockSpec(memory_space=pl.ANY)] * rows
            + [pl.BlockSpec((depth, tile), lambda i, *_: (0, first + i))]
            + [pl.BlockSpec((half, tile), lambda i, *_: (0, i))] * len(pieces)
            + [pl.BlockSpec((length, tile), lambda i, *_: (0, first + i))],
            out_specs=[pl.BlockSpec((span, tile), lambda i, *_: (0, i))] * rows,
            scratch_shapes=[
                pltpu.VMEM((2 * rows, length, half), jnp.bfloat16),
                pltpu.SemaphoreType.DMA((rows, 2)),
            ],
        ),
        out_shape=[jax.ShapeDtypeStruct((span, width), jnp.bfloat16)] * rows,
        compiler_params=pltpu.CompilerParams(vmem_limit_bytes=VMEM_BYTES),
        cost_estimate=pl.CostEstimate(
            flops=2 * length * depth * rows * width, bytes_accessed=12_000_000, transcendentals=0
        ),
        name="project",
    )(place, *heads, out_weight, *pieces, resid)


def settle_kernel(rows, place_ref, counts_ref, plan_ref, *refs):
    block_refs = refs[:rows]
    out_ref = refs[-1]
    my_row = place_ref[0]
    tokens, span = out_ref.shape[0], block_refs[0].shape[0]
    token = lax.broadcasted_iota(jnp.int32, (tokens, span), 0)
    slot = lax.broadcasted_iota(jnp.int32, (tokens, span), 1)
    sizes = [image_for(counts_ref, plan_ref, r, my_row, rows)[2] for r in range(rows)]
    total = None
    for k in range(rows):
        source = lax.rem(my_row - k + rows, rows)
        start, size = 0, 0
        for r in range(rows):
            start = start + jnp.where(r < source, sizes[r], 0)
            size = jnp.where(r == source, sizes[r], size)
        select = ((token - slot == start) & (slot < size)).astype(jnp.float32).astype(jnp.bfloat16)
        term = dot32(select, block_refs[k][...])
        total = term if total is None else total + term
    out_ref[...] = total.astype(jnp.bfloat16)


def settle(place, counts, plan, blocks, chunk, features, earlier):
    rows = len(blocks)
    span, width = blocks[0].shape
    tile = 256
    tiles = width // tile
    first = chunk * tiles
    more = [] if earlier is None else [earlier]
    return pl.pallas_call(
        lambda *refs: settle_kernel(rows, *refs),
        grid_spec=pltpu.PrefetchScalarGridSpec(
            num_scalar_prefetch=3,
            grid=(tiles,),
            in_specs=[pl.BlockSpec((span, tile), lambda i, *_: (0, i))] * rows
            + [pl.BlockSpec(memory_space=pl.ANY)] * len(more),
            out_specs=pl.BlockSpec((TOK, tile), lambda i, *_: (0, first + i)),
        ),
        out_shape=jax.ShapeDtypeStruct((TOK, features), jnp.bfloat16),
        input_output_aliases={3 + rows: 0} if more else {},
        compiler_params=pltpu.CompilerParams(vmem_limit_bytes=VMEM_BYTES),
        cost_estimate=pl.CostEstimate(
            flops=2 * TOK * rows * span * width, bytes_accessed=2_000_000, transcendentals=0
        ),
        name="settle",
    )(place, counts, plan, *blocks, *more)


def on_device_rings(
    qkv_home,
    resid_home,
    out_weight,
    label_weight,
    label_bias,
    query_gain,
    key_gain,
    patch_counts,
    move_plan,
    segment_ids,
):
    rows = lax.axis_size("dp")
    parts = lax.axis_size("mp")
    sharers = lax.axis_size("groups")
    my_row = lax.axis_index("dp")
    my_part = lax.axis_index("mp")
    my_group = lax.axis_index("groups")
    slots = segment_ids.shape[1]
    span = -(-(slots // rows) // 16) * 16
    padded = -(-slots // 16) * 16 + span
    depth, features = out_weight.shape
    half = depth // sharers
    width = features // CHUNKS
    image_ids = jnp.arange(rows, dtype=jnp.int32)
    place = jnp.stack([my_row, my_part, my_group]).astype(jnp.int32)

    mine = lax.dynamic_slice_in_dim(out_weight, my_group * half, half, 0)
    moving = [mine[:, c * width : (c + 1) * width] for c in range(CHUNKS)]
    pieces = [[] for _ in range(CHUNKS)]
    for _ in range(1, rows):
        for c in range(CHUNKS):
            moving[c] = lax.ppermute(moving[c], "dp", shifted(rows, 1))
            other = lax.ppermute(moving[c], "groups", crossed(sharers, 1))
            pieces[c] += [moving[c], other]

    qkv = jnp.pad(jnp.transpose(qkv_home[0], (1, 0, 2)), ((0, 0), (0, padded - slots), (0, 0)))
    heads, resid, head_means, resid_means = attend(
        place,
        patch_counts,
        move_plan,
        qkv,
        jnp.pad(resid_home[0], ((0, padded - slots), (0, 0))),
        query_gain[None],
        key_gain[None],
        span,
        [pieces[0][0]],
    )
    across = lax.ppermute(heads, "mp", crossed(parts, 2))
    beside = lax.ppermute(heads, "mp", crossed(parts, 1))
    beyond = lax.ppermute(across, "mp", crossed(parts, 1))

    got = lax.all_gather(head_means, ("dp", "mp"), axis=0)
    got = at(got.reshape(rows, parts, rows, depth), my_row, 1).reshape(rows * rows, depth)
    share = dot32(got, out_weight).reshape(rows, rows, features)
    share = share + jnp.where((image_ids == my_row)[:, None, None], resid_means[None], 0.0)
    share = share.reshape(rows * rows, features).astype(jnp.bfloat16)
    pooled = jnp.sum(lax.all_gather(share, "dp", axis=0).astype(jnp.float32), axis=0)
    terms = dot32(pooled.astype(jnp.bfloat16), label_weight)
    classes = label_weight.shape[1]
    terms = terms.reshape(rows, rows, classes).astype(jnp.bfloat16)
    terms = lax.all_to_all(terms, "mp", split_axis=1, concat_axis=1, tiled=True)
    logits = jnp.sum(terms.astype(jnp.float32), axis=1)
    probs = jax.nn.sigmoid(logits + label_bias[None, :]).astype(jnp.bfloat16)
    labels = lax.all_to_all(probs, "dp", split_axis=0, concat_axis=0, tiled=True)
    labels = labels.reshape(1, 1, rows * classes).astype(jnp.float32)

    mixed = None
    for c in range(CHUNKS):
        blocks = project(
            place, [heads, beside, across, beyond], out_weight, pieces[c], resid, c, width, span
        )
        arrived = [blocks[0]]
        for k in range(1, rows):
            arrived.append(lax.ppermute(blocks[k], "dp", shifted(rows, k)))
        mixed = settle(place, patch_counts, move_plan, arrived, c, features, mixed)
    return (mixed[None], labels)

def attend_home(qkv_rows, seg_rows, query_gain, key_gain):
    length = qkv_rows.shape[0]
    head_width = query_gain.shape[0]
    head_count = qkv_rows.shape[2] // head_width
    split_parts = qkv_rows.reshape(length, 3, head_count, head_width)
    queries = head_norm(split_parts[:, 0].astype(jnp.float32), query_gain).astype(jnp.bfloat16)
    key_rows = head_norm(split_parts[:, 1].astype(jnp.float32), key_gain).astype(jnp.bfloat16)
    scores = jnp.einsum(
        "qhd,khd->hqk", queries, key_rows, preferred_element_type=jnp.float32
    ) / math.sqrt(head_width)
    same_image = seg_rows[:, None] == seg_rows[None, :]
    raised = jnp.where(same_image[None], jnp.exp(scores), 0.0)
    weights = (raised / jnp.sum(raised, axis=-1, keepdims=True)).astype(jnp.bfloat16)
    head_out = jnp.einsum(
        "hqk,khd->qhd", weights, split_parts[:, 2], preferred_element_type=jnp.float32
    )
    return head_out.reshape(length, head_count * head_width).astype(jnp.bfloat16)


def project_home(heads_local, resid_rows, out_weight):
    gathered = lax.all_gather(heads_local, "mp", axis=1, tiled=True)
    running = resid_rows.astype(jnp.float32) + jnp.dot(
        gathered,
        lax.all_gather(out_weight, "dp", axis=0, tiled=True),
        preferred_element_type=jnp.float32,
    )
    return running.astype(jnp.bfloat16)


def pool(row_mixed, seg_rows, count_row):
    images = count_row.shape[0]
    member_ids = lax.broadcasted_iota(jnp.int32, (images, seg_rows.shape[0]), 0)
    member = (member_ids == seg_rows[None, :]).astype(jnp.bfloat16)
    image_sums = jnp.dot(member, row_mixed, preferred_element_type=jnp.float32)
    return (image_sums / count_row[:, None].astype(jnp.float32)).astype(jnp.bfloat16)


def label_terms(pooled, label_weight):
    return jnp.einsum(
        "abd,dc->abc",
        lax.all_gather(pooled[None], "dp", axis=0, tiled=True),
        label_weight,
        preferred_element_type=jnp.float32,
    )


def pick(values, row_index, is_valid):
    taken = jnp.take(values, row_index, axis=0)
    taken = taken.reshape(is_valid.shape + values.shape[1:])
    keep_mask = is_valid.reshape(is_valid.shape + (1,) * (values.ndim - 1))
    return jnp.where(keep_mask, taken, jnp.zeros_like(taken))


def on_device(
    qkv_home,
    resid_home,
    out_weight,
    label_weight,
    label_bias,
    query_gain,
    key_gain,
    patch_counts,
    move_plan,
    segment_ids,
):
    row_count = lax.axis_size("dp")
    my_index = lax.axis_index("dp")
    home_slots = segment_ids.shape[1]
    pair_slots = home_slots // row_count
    image_ids = lax.broadcasted_iota(jnp.int32, (row_count, row_count, row_count), 2)
    image_ends = jnp.cumsum(patch_counts, axis=1)
    starts = image_ends - patch_counts
    matches = (move_plan[:, :, None] == image_ids).astype(jnp.int32)
    image_sizes = jnp.sum(patch_counts[:, :, None] * matches, axis=1)
    firsts = jnp.sum(starts[:, :, None] * matches, axis=1)
    send_sizes = lax.dynamic_index_in_dim(image_sizes, my_index, 0, keepdims=False)
    send_firsts = lax.dynamic_index_in_dim(firsts, my_index, 0, keepdims=False)
    within = lax.broadcasted_iota(jnp.int32, (row_count, pair_slots), 1)
    send_valid = within < send_sizes[:, None]
    send_index = jnp.minimum(send_firsts[:, None] + within, home_slots - 1).reshape(-1)
    arrive_sizes = lax.dynamic_index_in_dim(image_sizes, my_index, 1, keepdims=False)
    arrive_ends = jnp.cumsum(arrive_sizes)
    arrive_starts = arrive_ends - arrive_sizes
    slot_grid = lax.broadcasted_iota(jnp.int32, (TOK, row_count), 0)
    source = jnp.sum((slot_grid >= arrive_ends[None, :]).astype(jnp.int32), axis=1)
    chosen = (source[:, None] == lax.broadcasted_iota(jnp.int32, (TOK, row_count), 1)).astype(
        jnp.int32
    )
    arrive_index = (
        source * pair_slots + slot_grid[:, 0] - jnp.sum(chosen * arrive_starts[None, :], axis=1)
    )
    home_mixed = project_home(
        attend_home(qkv_home[0], segment_ids[0], query_gain, key_gain), resid_home[0], out_weight
    )
    count_row = lax.dynamic_index_in_dim(patch_counts, my_index, 0, keepdims=False)
    pooled = pool(home_mixed, segment_ids[0], count_row)
    partial_value = label_terms(pooled, label_weight)
    send_mixed = pick(home_mixed, send_index, send_valid)
    got_mixed = lax.all_to_all(send_mixed, "dp", split_axis=0, concat_axis=0, tiled=True)
    mixed = jnp.take(got_mixed.reshape(row_count * pair_slots, -1), arrive_index, axis=0)
    logit_sums = lax.psum_scatter(
        partial_value.astype(jnp.bfloat16), "mp", scatter_dimension=1, tiled=True
    ).astype(jnp.float32)
    class_probs = jax.nn.sigmoid(logit_sums + label_bias[None, None, :])
    labels = lax.all_to_all(
        class_probs.astype(jnp.bfloat16), "dp", split_axis=0, concat_axis=2, tiled=True
    ).astype(class_probs.dtype)
    return (mixed[None], labels)

def solution(mesh):
    rows, parts, sharers = (mesh.shape[name] for name in ("dp", "mp", "groups"))
    small = rows == parts == 4 and sharers == 2
    return jax.shard_map(
        on_device_rings if small else on_device,
        mesh=mesh,
        in_specs=(
            P(("groups", "dp"), None, None, "mp"),
            P(("groups", "dp"), None, "mp"),
            P("dp", "mp"),
            P("mp", "dp"),
            P("dp"),
            P(),
            P(),
            P("groups", None),
            P("groups", None),
            P(("groups", "dp"), None),
        ),
        out_specs=(P(("groups", "dp"), None, "mp"), P(("groups", "dp"), "mp", None)),
        check_vma=False,
    )
```

```python
import math

import jax
import jax.numpy as jnp
from jax import lax
from jax.experimental import pallas as pl
from jax.experimental.pallas import tpu as pltpu
from jax.sharding import PartitionSpec as P

TOK = 384
CHUNKS = 2
VMEM_BYTES = 48 * 1024 * 1024


EPSILON = 1e-06


def head_norm(values, norm_gain):
    center = values - jnp.mean(values, axis=-1, keepdims=True)
    spread = jnp.mean(center * center, axis=-1, keepdims=True)
    return center * lax.rsqrt(spread + EPSILON) * norm_gain


def shifted(count, by):
    return [(i, (i + by) % count) for i in range(count)]


def crossed(count, by):
    return [(i, i ^ by) for i in range(count)]


def send(values, axis, pairs, name):
    with jax.named_scope(name):
        return lax.ppermute(values, axis, pairs)


def dot32(left, right):
    return jnp.dot(left, right, preferred_element_type=jnp.float32)


def at(values, index, axis=0):
    return lax.dynamic_index_in_dim(values, index, axis, keepdims=False)


def image_for(counts_ref, plan_ref, row, dest, images):
    image, first, size, before = 0, 0, 0, 0
    for j in range(images):
        count = counts_ref[row, j]
        hit = plan_ref[row, j] == dest
        image = jnp.where(hit, j, image)
        first = jnp.where(hit, before, first)
        size = jnp.where(hit, count, size)
        before = before + count
    return image, first, size


def attend_kernel(
    rows,
    span,
    place_ref,
    counts_ref,
    plan_ref,
    qkv_ref,
    resid_ref,
    query_gain_ref,
    key_gain_ref,
    *rest,
):
    heads_ref, sent_ref, resid_means_ref, means_ref = rest[-4:]
    k = pl.program_id(0)
    lines = pl.ds(pl.multiple_of(k * span, 16), span)
    my_row = place_ref[0]
    image, first, size = image_for(
        counts_ref, plan_ref, my_row, lax.rem(my_row + k, rows), rows
    )
    window = span + 16
    begin = pl.multiple_of(first // 16 * 16, 16)
    shift = first - begin
    taken = lax.broadcasted_iota(jnp.int32, (span, window), 0)
    slot = lax.broadcasted_iota(jnp.int32, (span, window), 1)
    select = ((slot - taken == shift) & (taken < size)).astype(jnp.float32).astype(jnp.bfloat16)
    count = size.astype(jnp.float32)
    resid = dot32(select, resid_ref[pl.ds(begin, window), :])
    sent_ref[...] = resid.astype(jnp.bfloat16)
    here = lax.broadcasted_iota(jnp.int32, (means_ref.shape[0], 1), 0) == image
    resid_mean = jnp.sum(resid, axis=0, keepdims=True) / count
    resid_means_ref[...] = jnp.where(here, resid_mean, resid_means_ref[...])

    @pl.when(k == 0)
    def _():
        means_ref[...] = jnp.zeros_like(means_ref)
    queries = dot32(select, qkv_ref[0, pl.ds(begin, window), :])
    keys = dot32(select, qkv_ref[1, pl.ds(begin, window), :])
    values = dot32(select, qkv_ref[2, pl.ds(begin, window), :]).astype(jnp.bfloat16)
    head_width = query_gain_ref.shape[1]
    inside = lax.broadcasted_iota(jnp.int32, (span, span), 1) < size
    kept = lax.broadcasted_iota(jnp.int32, (span, 1), 0) < size
    for h in range(heads_ref.shape[1] // head_width):
        columns = slice(h * head_width, (h + 1) * head_width)
        query = head_norm(queries[:, columns], query_gain_ref[...]).astype(jnp.bfloat16)
        key = head_norm(keys[:, columns], key_gain_ref[...]).astype(jnp.bfloat16)
        scores = lax.dot_general(
            query, key, (((1,), (1,)), ((), ())), preferred_element_type=jnp.float32
        ) * (1.0 / math.sqrt(head_width))
        raised = jnp.where(inside, jnp.exp(scores), 0.0)
        scale = jnp.where(kept, 1.0 / jnp.sum(raised, axis=-1, keepdims=True), 0.0)
        weights = (raised * scale).astype(jnp.bfloat16)
        head = dot32(weights, values[:, columns]).astype(jnp.bfloat16)
        heads_ref[lines, columns] = head
        head_mean = jnp.sum(head.astype(jnp.float32), axis=0, keepdims=True) / count
        means_ref[:, columns] = jnp.where(here, head_mean, means_ref[:, columns])

    @pl.when(k == rows - 1)
    def _():
        heads_ref[rows * span :, :] = means_ref[...].astype(jnp.bfloat16)


def attend(place, counts, plan, qkv, resid, query_gain, key_gain, span, after):
    rows = counts.shape[0]
    local, features = qkv.shape[2], resid.shape[1]
    extra = -(-rows // 16) * 16
    fixed = lambda shape: pl.BlockSpec(shape, lambda k, *_: (0,) * len(shape))
    return pl.pallas_call(
        lambda *refs: attend_kernel(rows, span, *refs),
        grid_spec=pltpu.PrefetchScalarGridSpec(
            num_scalar_prefetch=3,
            grid=(rows,),
            in_specs=[fixed(x.shape) for x in (qkv, resid, query_gain, key_gain)]
            + [pl.BlockSpec(memory_space=pl.ANY)] * len(after),
            out_specs=[
                fixed((rows * span + extra, local)),
                pl.BlockSpec((span, features), lambda k, *_: (k, 0)),
                fixed((extra, features)),
            ],
            scratch_shapes=[pltpu.VMEM((extra, local), jnp.float32)],
        ),
        out_shape=[
            jax.ShapeDtypeStruct((rows * span + extra, local), jnp.bfloat16),
            jax.ShapeDtypeStruct((rows * span, features), jnp.bfloat16),
            jax.ShapeDtypeStruct((extra, features), jnp.float32),
        ],
        compiler_params=pltpu.CompilerParams(vmem_limit_bytes=VMEM_BYTES),
        cost_estimate=pl.CostEstimate(
            flops=10_000_000_000, bytes_accessed=12_000_000, transcendentals=0
        ),
        name="attend",
    )(place, counts, plan, qkv, resid, query_gain, key_gain, *after)


def early_kernel(rows, chunks, place_ref, *refs):
    head_refs = refs[:rows]
    own_ref = refs[rows]
    piece_refs = refs[rows + 1 : rows + 1 + 3 * chunks]
    resid_ref, total_ref, late_ref = refs[rows + 1 + 3 * chunks :][:3]
    held_ref, weight_ref, head_sems, weight_sems, late_sem = refs[-5:]
    my_row, my_part, my_group = place_ref[0], place_ref[1], place_ref[2]
    tiles, used, tile = weight_ref.shape
    depth = held_ref.shape[1] // rows
    half = depth // 2

    def head_copies():
        copies = []
        for x in range(rows):
            step = lax.rem(my_row - (x ^ my_part) + rows, rows)
            for s in range(2):
                turned = jnp.where(step == 0, s, s ^ my_group)
                start = pl.multiple_of(step * depth + turned * half, 128)
                copies.append(
                    pltpu.make_async_copy(
                        head_refs[x].at[: held_ref.shape[0], s * half : (s + 1) * half],
                        held_ref.at[:, pl.ds(start, half)],
                        head_sems.at[x, s],
                    )
                )
        return copies

    def weight_copies(i):
        chunk, column = i * chunks // tiles, i % (tiles // chunks) * tile
        sources = [own_ref.at[:, i * tile : (i + 1) * tile]]
        sources += [piece_refs[3 * chunk + n].at[:, column : column + tile] for n in range(3)]
        starts = [0, depth, depth + half, depth + 2 * half]
        return [
            pltpu.make_async_copy(
                source, weight_ref.at[i, pl.ds(start, source.shape[0])], weight_sems.at[i, n]
            )
            for n, (source, start) in enumerate(zip(sources, starts))
        ]

    i = pl.program_id(0)
    late_copy = pltpu.make_async_copy(held_ref.at[:, used:], late_ref, late_sem)

    @pl.when(i == 0)
    def _():
        for copy in head_copies():
            copy.start()
        for j in range(tiles):
            for copy in weight_copies(j):
                copy.start()
        for copy in head_copies():
            copy.wait()
        late_copy.start()

    for j in range(tiles):

        @pl.when(i == j)
        def _():
            for copy in weight_copies(j):
                copy.wait()

    length = resid_ref.shape[0]
    for start in range(0, length, 256):
        lines = slice(start, min(start + 256, length))
        total = dot32(held_ref[lines, :used], weight_ref[i])
        total_ref[lines] = total + resid_ref[lines].astype(jnp.float32)

    @pl.when(i == tiles - 1)
    def _():
        late_copy.wait()


def project_early(place, heads, out_weight, pieces, resid):
    rows, chunks = len(heads), len(pieces)
    length, features = resid.shape
    depth = heads[0].shape[1]
    used = depth * 5 // 2
    tile = 256
    tiles = features // tile
    flat = [piece for chunk in pieces for piece in chunk[:3]]
    anywhere = pl.BlockSpec(memory_space=pl.ANY)
    column = lambda x: pl.BlockSpec((x, tile), lambda i: (0, i))
    return pl.pallas_call(
        lambda *refs: early_kernel(rows, chunks, *refs),
        grid=(tiles,),
        in_specs=[pl.BlockSpec(memory_space=pltpu.SMEM)]
        + [anywhere] * (rows + 1 + len(flat))
        + [column(length)],
        out_specs=[column(length), anywhere],
        scratch_shapes=[
            pltpu.VMEM((length, rows * depth), jnp.bfloat16),
            pltpu.VMEM((tiles, used, tile), jnp.bfloat16),
            pltpu.SemaphoreType.DMA((rows, 2)),
            pltpu.SemaphoreType.DMA((tiles, 4)),
            pltpu.SemaphoreType.DMA,
        ],
        out_shape=[
            jax.ShapeDtypeStruct((length, features), jnp.float32),
            jax.ShapeDtypeStruct((length, rows * depth - used), jnp.bfloat16),
        ],
        compiler_params=pltpu.CompilerParams(vmem_limit_bytes=VMEM_BYTES),
        cost_estimate=pl.CostEstimate(
            flops=2 * length * used * features, bytes_accessed=12_000_000, transcendentals=0
        ),
        name="project_early",
    )(place, *heads, out_weight, *flat, resid)


def late_kernel(rows, total_ref, late_ref, *refs):
    piece_refs, out_refs = refs[:3], refs[-rows:]
    half = piece_refs[0].shape[0]
    span = out_refs[0].shape[0]
    for k in range(rows):
        lines = slice(k * span, (k + 1) * span)
        total = total_ref[lines, :]
        for n in range(3):
            total = total + dot32(late_ref[lines, n * half : (n + 1) * half], piece_refs[n][...])
        out_refs[k][...] = total.astype(jnp.bfloat16)


def project_late(total, late, pieces, chunk, rows, span, after):
    half, width = pieces[0].shape
    length = total.shape[0]
    tile = 256
    tiles = width // tile
    first = chunk * tiles
    return pl.pallas_call(
        lambda *refs: late_kernel(rows, *refs),
        grid=(tiles,),
        in_specs=[
            pl.BlockSpec((length, tile), lambda i: (0, first + i)),
            pl.BlockSpec(late.shape, lambda i: (0, 0)),
        ]
        + [pl.BlockSpec((half, tile), lambda i: (0, i))] * 3
        + [pl.BlockSpec(memory_space=pl.ANY)] * len(after),
        out_specs=[pl.BlockSpec((span, tile), lambda i: (0, i))] * rows,
        out_shape=[jax.ShapeDtypeStruct((span, width), jnp.bfloat16)] * rows,
        compiler_params=pltpu.CompilerParams(vmem_limit_bytes=VMEM_BYTES),
        cost_estimate=pl.CostEstimate(
            flops=6 * length * half * width, bytes_accessed=6_000_000, transcendentals=0
        ),
        name="project_late",
    )(total, late, *pieces, *after)


def one_hot(hits):
    return hits.astype(jnp.float32).astype(jnp.bfloat16)


def parts_kernel(rows, start, place_ref, *refs):
    head_refs, out_refs = refs[:rows], refs[rows : 2 * rows]
    tail_ref, sems = refs[2 * rows :]
    copies = [
        pltpu.make_async_copy(
            head_refs[x].at[start : start + tail_ref.shape[1]], tail_ref.at[x], sems.at[x]
        )
        for x in range(rows)
    ]
    for copy in copies:
        copy.start()
    for copy in copies:
        copy.wait()
    for k in range(rows):
        row = lax.rem(place_ref[0] + k, rows)
        out_refs[k][...] = tail_ref[row ^ place_ref[1]][:rows]


def head_parts(place, heads, start):
    rows, (length, depth) = len(heads), heads[0].shape
    return pl.pallas_call(
        lambda *refs: parts_kernel(rows, start, *refs),
        in_specs=[pl.BlockSpec(memory_space=pltpu.SMEM)]
        + [pl.BlockSpec(memory_space=pl.ANY)] * rows,
        out_specs=[pl.BlockSpec(memory_space=pltpu.VMEM)] * rows,
        out_shape=[jax.ShapeDtypeStruct((rows, depth), jnp.bfloat16)] * rows,
        scratch_shapes=[
            pltpu.VMEM((rows, length - start, depth), jnp.bfloat16),
            pltpu.SemaphoreType.DMA((rows,)),
        ],
        cost_estimate=pl.CostEstimate(flops=1000, bytes_accessed=1000, transcendentals=0),
        compiler_params=pltpu.CompilerParams(vmem_limit_bytes=VMEM_BYTES),
        name="head_parts",
    )(place, *heads)


def share_kernel(rows, place_ref, *refs):
    got_refs = refs[:rows]
    weight_ref, resid_ref = refs[rows : rows + 2]
    share_ref = refs[-1]
    my_row = place_ref[0]
    count = rows * rows
    image = lax.broadcasted_iota(jnp.int32, (count, rows), 0)
    entry = lax.broadcasted_iota(jnp.int32, (count, rows), 1)
    got = None
    for k in range(rows):
        row = lax.rem(my_row - k + rows, rows)
        term = dot32(one_hot(image == row * rows + entry), got_refs[k][...])
        got = term if got is None else got + term
    mine = lax.broadcasted_iota(jnp.int32, (count, 1), 0) // rows == my_row
    resid = jnp.concatenate([resid_ref[:rows]] * rows, axis=0)
    share = dot32(got.astype(jnp.bfloat16), weight_ref[...]) + jnp.where(mine, resid, 0.0)
    share_ref[...] = share.astype(jnp.bfloat16)


def local_call(kernel, out_shape, operands, after, place, name, flops):
    whole = pl.BlockSpec(memory_space=pltpu.VMEM)
    return pl.pallas_call(
        kernel,
        in_specs=[pl.BlockSpec(memory_space=pltpu.SMEM)]
        + [whole] * len(operands)
        + [pl.BlockSpec(memory_space=pl.ANY)] * len(after),
        out_specs=jax.tree.map(lambda _: whole, out_shape),
        out_shape=out_shape,
        compiler_params=pltpu.CompilerParams(vmem_limit_bytes=VMEM_BYTES),
        cost_estimate=pl.CostEstimate(flops=flops, bytes_accessed=1000, transcendentals=0),
        name=name,
    )(place, *operands, *after)


def after_all(values, after):
    return lax.optimization_barrier((list(values), list(after)))[0]


def terms_kernel(rows, place_ref, *refs):
    share_refs = refs[:rows]
    weight_ref = refs[rows]
    out_refs = refs[-rows - 1 : -1]
    pooled_ref = refs[-1]
    count = rows * rows

    @pl.when(pl.program_id(0) == 0)
    def _():
        pooled = share_refs[0][...].astype(jnp.float32)
        for k in range(1, rows):
            pooled = pooled + share_refs[k][...].astype(jnp.float32)
        wanted = lax.broadcasted_iota(jnp.int32, (count, count), 0)
        image = lax.broadcasted_iota(jnp.int32, (count, count), 1)
        part = wanted // rows ^ place_ref[1]
        order = one_hot(image == wanted % rows * rows + part)
        pooled_ref[...] = dot32(order, pooled.astype(jnp.bfloat16)).astype(jnp.bfloat16)

    terms = dot32(pooled_ref[...], weight_ref[...]).astype(jnp.bfloat16)
    for k in range(rows):
        out_refs[k][...] = terms[k * rows : (k + 1) * rows]


def label_terms_by_part(place, shares, label_weight, after):
    rows = len(shares)
    count, features = shares[0].shape
    classes = label_weight.shape[1]
    tile = 512
    fixed = pl.BlockSpec((count, features), lambda i, *_: (0, 0))
    return pl.pallas_call(
        lambda *refs: terms_kernel(rows, *refs),
        grid_spec=pltpu.PrefetchScalarGridSpec(
            num_scalar_prefetch=1,
            grid=(classes // tile,),
            in_specs=[fixed] * rows
            + [pl.BlockSpec((features, tile), lambda i, *_: (0, i))]
            + [pl.BlockSpec(memory_space=pl.ANY)] * len(after),
            out_specs=[pl.BlockSpec((rows, tile), lambda i, *_: (0, i))] * rows,
            scratch_shapes=[pltpu.VMEM((count, features), jnp.bfloat16)],
        ),
        out_shape=[jax.ShapeDtypeStruct((rows, classes), jnp.bfloat16)] * rows,
        compiler_params=pltpu.CompilerParams(vmem_limit_bytes=VMEM_BYTES),
        cost_estimate=pl.CostEstimate(
            flops=2 * count * features * classes, bytes_accessed=12_000_000, transcendentals=0
        ),
        name="label_terms",
    )(place, *shares, label_weight, *after)


def probs_kernel(rows, place_ref, *refs):
    term_refs = refs[:rows]
    bias_ref = refs[rows]
    out_refs = refs[-rows:]
    logits = term_refs[0][...].astype(jnp.float32)
    for k in range(1, rows):
        logits = logits + term_refs[k][...].astype(jnp.float32)
    probs = jax.nn.sigmoid(logits + bias_ref[...])
    line = lax.broadcasted_iota(jnp.int32, (rows, 1), 0)
    for k in range(rows):
        row = lax.rem(place_ref[0] + k, rows)
        picked = jnp.sum(jnp.where(line == row, probs, 0.0), axis=0, keepdims=True)
        out_refs[k][...] = picked.astype(jnp.bfloat16)


def labels_kernel(rows, place_ref, *refs):
    out_ref = refs[-1]
    classes = refs[0].shape[1]
    for k in range(rows):
        row = lax.rem(place_ref[0] - k + rows, rows)
        columns = pl.ds(pl.multiple_of(row * classes, 128), classes)
        out_ref[:, columns] = refs[k][...].astype(jnp.float32)


def settle_kernel(rows, place_ref, counts_ref, plan_ref, *refs):
    block_refs = refs[:rows]
    out_ref = refs[-1]
    my_row = place_ref[0]
    tokens, span = out_ref.shape[0], block_refs[0].shape[0]
    token = lax.broadcasted_iota(jnp.int32, (tokens, span), 0)
    slot = lax.broadcasted_iota(jnp.int32, (tokens, span), 1)
    sizes = [image_for(counts_ref, plan_ref, r, my_row, rows)[2] for r in range(rows)]
    total = None
    for k in range(rows):
        source = lax.rem(my_row - k + rows, rows)
        start, size = 0, 0
        for r in range(rows):
            start = start + jnp.where(r < source, sizes[r], 0)
            size = jnp.where(r == source, sizes[r], size)
        select = ((token - slot == start) & (slot < size)).astype(jnp.float32).astype(jnp.bfloat16)
        term = dot32(select, block_refs[k][...])
        total = term if total is None else total + term
    out_ref[...] = total.astype(jnp.bfloat16)


def settle(place, counts, plan, blocks, chunk, features, earlier, after):
    rows = len(blocks)
    span, width = blocks[0].shape
    tile = 256
    tiles = width // tile
    first = chunk * tiles
    more = [] if earlier is None else [earlier]
    return pl.pallas_call(
        lambda *refs: settle_kernel(rows, *refs),
        grid_spec=pltpu.PrefetchScalarGridSpec(
            num_scalar_prefetch=3,
            grid=(tiles,),
            in_specs=[pl.BlockSpec((span, tile), lambda i, *_: (0, i))] * rows
            + [pl.BlockSpec(memory_space=pl.ANY)] * (len(more) + len(after)),
            out_specs=pl.BlockSpec((TOK, tile), lambda i, *_: (0, first + i)),
        ),
        out_shape=jax.ShapeDtypeStruct((TOK, features), jnp.bfloat16),
        input_output_aliases={3 + rows: 0} if more else {},
        compiler_params=pltpu.CompilerParams(vmem_limit_bytes=VMEM_BYTES),
        cost_estimate=pl.CostEstimate(
            flops=2 * TOK * rows * span * width, bytes_accessed=2_000_000, transcendentals=0
        ),
        name="settle",
    )(place, counts, plan, *blocks, *more, *after)


def on_device_rings(
    qkv_home,
    resid_home,
    out_weight,
    label_weight,
    label_bias,
    query_gain,
    key_gain,
    patch_counts,
    move_plan,
    segment_ids,
):
    rows = lax.axis_size("dp")
    parts = lax.axis_size("mp")
    sharers = lax.axis_size("groups")
    my_row = lax.axis_index("dp")
    my_part = lax.axis_index("mp")
    my_group = lax.axis_index("groups")
    slots = segment_ids.shape[1]
    span = -(-(slots // rows) // 16) * 16
    padded = -(-slots // 16) * 16 + span
    depth, features = out_weight.shape
    half = depth // sharers
    width = features // CHUNKS
    place = jnp.stack([my_row, my_part, my_group]).astype(jnp.int32)

    mine = lax.dynamic_slice_in_dim(out_weight, my_group * half, half, 0)
    moving = [mine[:, c * width : (c + 1) * width] for c in range(CHUNKS)]
    moving = [send(x, "dp", shifted(rows, 1), f"w{c}_1") for c, x in enumerate(moving)]

    qkv = jnp.pad(jnp.transpose(qkv_home[0], (1, 0, 2)), ((0, 0), (0, padded - slots), (0, 0)))
    heads, resid, resid_means = attend(
        place,
        patch_counts,
        move_plan,
        qkv,
        jnp.pad(resid_home[0], ((0, padded - slots), (0, 0))),
        query_gain[None],
        key_gain[None],
        span,
        moving[:1],
    )
    heads = after_all([heads], moving[1:])[0]
    across = send(heads, "mp", crossed(parts, 2), "h_2")
    beside = send(heads, "mp", crossed(parts, 1), "h_1")

    following = [send(x, "dp", shifted(rows, 1), f"w{c}_2") for c, x in enumerate(moving)]
    others = [
        send(x, "groups", crossed(sharers, 1), f"y{c}_1") for c, x in enumerate(moving)
    ]
    pieces = [[x, y, z] for x, y, z in zip(moving, others, following)]
    turned = after_all([across], [*following, *others])[0]
    beyond = send(turned, "mp", crossed(parts, 1), "h_3")
    every_head = [heads, beside, across, beyond]

    gathered = head_parts(place, every_head, rows * span)
    gathered = [gathered[0]] + [
        send(gathered[k], "dp", shifted(rows, k), f"g_{k}") for k in range(1, rows)
    ]
    image_count = rows * rows
    share = local_call(
        lambda *refs: share_kernel(rows, *refs),
        jax.ShapeDtypeStruct((image_count, features), jnp.bfloat16),
        [*gathered, out_weight, resid_means],
        [],
        place,
        "share",
        1000,
    )
    shares = [share] + [send(share, "dp", shifted(rows, k), f"s_{k}") for k in range(1, rows)]

    total, late = project_early(place, every_head, out_weight, pieces, resid)
    pieces, moving = [], following
    for c in range(CHUNKS):
        x = after_all([moving[c]], [total, *gathered[1:]])[0] if c else moving[c]
        x = send(x, "dp", shifted(rows, 1), f"w{c}_3")
        y = after_all([moving[c]], [x, *shares[1:]])[0] if c else moving[c]
        y = send(y, "groups", crossed(sharers, 1), f"y{c}_2")
        z = after_all([x], [y, total, share])[0] if c == 0 else x
        z = send(z, "groups", crossed(sharers, 1), f"y{c}_3")
        pieces.append([y, x, z])

    classes = label_weight.shape[1]
    arrived = []
    for c in range(CHUNKS):
        after = [terms[0], arrived[0][3]] if c else shares[1:]
        blocks = project_late(total, late, pieces[c], c, rows, span, after)
        arrived.append(
            [blocks[0]] + [send(blocks[k], "dp", shifted(rows, k), f"m{c}_{k}") for k in range(1, rows)]
        )
        if c == 0:
            terms = label_terms_by_part(place, shares, label_weight, arrived[0][1:2])

    terms = [terms[0]] + [
        send(terms[k], "mp", crossed(parts, k), f"t_{k}") for k in range(1, parts)
    ]
    probs = local_call(
        lambda *refs: probs_kernel(rows, *refs),
        [jax.ShapeDtypeStruct((1, classes), jnp.bfloat16)] * rows,
        [*terms, label_bias[None]],
        [],
        place,
        "probs",
        1000,
    )
    probs = [probs[0]] + [send(probs[k], "dp", shifted(rows, k), f"l_{k}") for k in range(1, rows)]
    labels = local_call(
        lambda *refs: labels_kernel(rows, *refs),
        jax.ShapeDtypeStruct((1, rows * classes), jnp.float32),
        probs,
        [],
        place,
        "labels",
        1000,
    )
    mixed = None
    for c in range(CHUNKS):
        after = [labels] if c == CHUNKS - 1 else []
        mixed = settle(place, patch_counts, move_plan, arrived[c], c, features, mixed, after)
    labels = labels[None]
    return (mixed[None], labels)

def attend_home(qkv_rows, seg_rows, query_gain, key_gain):
    length = qkv_rows.shape[0]
    head_width = query_gain.shape[0]
    head_count = qkv_rows.shape[2] // head_width
    split_parts = qkv_rows.reshape(length, 3, head_count, head_width)
    queries = head_norm(split_parts[:, 0].astype(jnp.float32), query_gain).astype(jnp.bfloat16)
    key_rows = head_norm(split_parts[:, 1].astype(jnp.float32), key_gain).astype(jnp.bfloat16)
    scores = jnp.einsum(
        "qhd,khd->hqk", queries, key_rows, preferred_element_type=jnp.float32
    ) / math.sqrt(head_width)
    same_image = seg_rows[:, None] == seg_rows[None, :]
    raised = jnp.where(same_image[None], jnp.exp(scores), 0.0)
    weights = (raised / jnp.sum(raised, axis=-1, keepdims=True)).astype(jnp.bfloat16)
    head_out = jnp.einsum(
        "hqk,khd->qhd", weights, split_parts[:, 2], preferred_element_type=jnp.float32
    )
    return head_out.reshape(length, head_count * head_width).astype(jnp.bfloat16)


def project_home(heads_local, resid_rows, out_weight):
    gathered = lax.all_gather(heads_local, "mp", axis=1, tiled=True)
    running = resid_rows.astype(jnp.float32) + jnp.dot(
        gathered,
        lax.all_gather(out_weight, "dp", axis=0, tiled=True),
        preferred_element_type=jnp.float32,
    )
    return running.astype(jnp.bfloat16)


def pool(row_mixed, seg_rows, count_row):
    images = count_row.shape[0]
    member_ids = lax.broadcasted_iota(jnp.int32, (images, seg_rows.shape[0]), 0)
    member = (member_ids == seg_rows[None, :]).astype(jnp.bfloat16)
    image_sums = jnp.dot(member, row_mixed, preferred_element_type=jnp.float32)
    return (image_sums / count_row[:, None].astype(jnp.float32)).astype(jnp.bfloat16)


def label_terms(pooled, label_weight):
    return jnp.einsum(
        "abd,dc->abc",
        lax.all_gather(pooled[None], "dp", axis=0, tiled=True),
        label_weight,
        preferred_element_type=jnp.float32,
    )


def pick(values, row_index, is_valid):
    taken = jnp.take(values, row_index, axis=0)
    taken = taken.reshape(is_valid.shape + values.shape[1:])
    keep_mask = is_valid.reshape(is_valid.shape + (1,) * (values.ndim - 1))
    return jnp.where(keep_mask, taken, jnp.zeros_like(taken))


def on_device(
    qkv_home,
    resid_home,
    out_weight,
    label_weight,
    label_bias,
    query_gain,
    key_gain,
    patch_counts,
    move_plan,
    segment_ids,
):
    row_count = lax.axis_size("dp")
    my_index = lax.axis_index("dp")
    home_slots = segment_ids.shape[1]
    pair_slots = home_slots // row_count
    image_ids = lax.broadcasted_iota(jnp.int32, (row_count, row_count, row_count), 2)
    image_ends = jnp.cumsum(patch_counts, axis=1)
    starts = image_ends - patch_counts
    matches = (move_plan[:, :, None] == image_ids).astype(jnp.int32)
    image_sizes = jnp.sum(patch_counts[:, :, None] * matches, axis=1)
    firsts = jnp.sum(starts[:, :, None] * matches, axis=1)
    send_sizes = lax.dynamic_index_in_dim(image_sizes, my_index, 0, keepdims=False)
    send_firsts = lax.dynamic_index_in_dim(firsts, my_index, 0, keepdims=False)
    within = lax.broadcasted_iota(jnp.int32, (row_count, pair_slots), 1)
    send_valid = within < send_sizes[:, None]
    send_index = jnp.minimum(send_firsts[:, None] + within, home_slots - 1).reshape(-1)
    arrive_sizes = lax.dynamic_index_in_dim(image_sizes, my_index, 1, keepdims=False)
    arrive_ends = jnp.cumsum(arrive_sizes)
    arrive_starts = arrive_ends - arrive_sizes
    slot_grid = lax.broadcasted_iota(jnp.int32, (TOK, row_count), 0)
    source = jnp.sum((slot_grid >= arrive_ends[None, :]).astype(jnp.int32), axis=1)
    chosen = (source[:, None] == lax.broadcasted_iota(jnp.int32, (TOK, row_count), 1)).astype(
        jnp.int32
    )
    arrive_index = (
        source * pair_slots + slot_grid[:, 0] - jnp.sum(chosen * arrive_starts[None, :], axis=1)
    )
    home_mixed = project_home(
        attend_home(qkv_home[0], segment_ids[0], query_gain, key_gain), resid_home[0], out_weight
    )
    count_row = lax.dynamic_index_in_dim(patch_counts, my_index, 0, keepdims=False)
    pooled = pool(home_mixed, segment_ids[0], count_row)
    partial_value = label_terms(pooled, label_weight)
    send_mixed = pick(home_mixed, send_index, send_valid)
    got_mixed = lax.all_to_all(send_mixed, "dp", split_axis=0, concat_axis=0, tiled=True)
    mixed = jnp.take(got_mixed.reshape(row_count * pair_slots, -1), arrive_index, axis=0)
    logit_sums = lax.psum_scatter(
        partial_value.astype(jnp.bfloat16), "mp", scatter_dimension=1, tiled=True
    ).astype(jnp.float32)
    class_probs = jax.nn.sigmoid(logit_sums + label_bias[None, None, :])
    labels = lax.all_to_all(
        class_probs.astype(jnp.bfloat16), "dp", split_axis=0, concat_axis=2, tiled=True
    ).astype(class_probs.dtype)
    return (mixed[None], labels)

def solution(mesh):
    rows, parts, sharers = (mesh.shape[name] for name in ("dp", "mp", "groups"))
    small = rows == parts == 4 and sharers == 2
    return jax.shard_map(
        on_device_rings if small else on_device,
        mesh=mesh,
        in_specs=(
            P(("groups", "dp"), None, None, "mp"),
            P(("groups", "dp"), None, "mp"),
            P("dp", "mp"),
            P("mp", "dp"),
            P("dp"),
            P(),
            P(),
            P("groups", None),
            P("groups", None),
            P(("groups", "dp"), None),
        ),
        out_specs=(P(("groups", "dp"), None, "mp"), P(("groups", "dp"), "mp", None)),
        check_vma=False,
    )
```

```python
import math

import jax
import jax.numpy as jnp
from jax import lax
from jax.experimental import pallas as pl
from jax.experimental.pallas import tpu as pltpu
from jax.sharding import PartitionSpec as P

TOK = 384
CHUNKS = 2
VMEM_BYTES = 24 * 1024 * 1024
EARLY_FLOPS = 4_000_000_000


EPSILON = 1e-06


def head_norm(values, norm_gain):
    center = values - jnp.mean(values, axis=-1, keepdims=True)
    spread = jnp.mean(center * center, axis=-1, keepdims=True)
    return center * lax.rsqrt(spread + EPSILON) * norm_gain


def shifted(count, by):
    return [(i, (i + by) % count) for i in range(count)]


def crossed(count, by):
    return [(i, i ^ by) for i in range(count)]


def send(values, axis, pairs, name):
    with jax.named_scope(name):
        return lax.ppermute(values, axis, pairs)


def dot32(left, right):
    return jnp.dot(left, right, preferred_element_type=jnp.float32)


def at(values, index, axis=0):
    return lax.dynamic_index_in_dim(values, index, axis, keepdims=False)


def image_for(counts_ref, plan_ref, row, dest, images):
    image, first, size, before = 0, 0, 0, 0
    for j in range(images):
        count = counts_ref[row, j]
        hit = plan_ref[row, j] == dest
        image = jnp.where(hit, j, image)
        first = jnp.where(hit, before, first)
        size = jnp.where(hit, count, size)
        before = before + count
    return image, first, size


def attend_kernel(
    rows,
    span,
    place_ref,
    counts_ref,
    plan_ref,
    qkv_ref,
    resid_ref,
    query_gain_ref,
    key_gain_ref,
    *rest,
):
    heads_ref, sent_ref, resid_means_ref, means_ref = rest[-4:]
    k = pl.program_id(0)
    lines = pl.ds(pl.multiple_of(k * span, 16), span)
    my_row = place_ref[0]
    image, first, size = image_for(
        counts_ref, plan_ref, my_row, lax.rem(my_row + k, rows), rows
    )
    window = span + 16
    begin = pl.multiple_of(first // 16 * 16, 16)
    shift = first - begin
    taken = lax.broadcasted_iota(jnp.int32, (span, window), 0)
    slot = lax.broadcasted_iota(jnp.int32, (span, window), 1)
    select = ((slot - taken == shift) & (taken < size)).astype(jnp.float32).astype(jnp.bfloat16)
    count = size.astype(jnp.float32)
    resid = dot32(select, resid_ref[pl.ds(begin, window), :])
    sent_ref[...] = resid.astype(jnp.bfloat16)
    here = lax.broadcasted_iota(jnp.int32, (means_ref.shape[0], 1), 0) == image
    resid_mean = jnp.sum(resid, axis=0, keepdims=True) / count
    resid_means_ref[...] = jnp.where(here, resid_mean, resid_means_ref[...])

    @pl.when(k == 0)
    def _():
        means_ref[...] = jnp.zeros_like(means_ref)
    queries = dot32(select, qkv_ref[0, pl.ds(begin, window), :])
    keys = dot32(select, qkv_ref[1, pl.ds(begin, window), :])
    values = dot32(select, qkv_ref[2, pl.ds(begin, window), :]).astype(jnp.bfloat16)
    head_width = query_gain_ref.shape[1]
    inside = lax.broadcasted_iota(jnp.int32, (span, span), 1) < size
    kept = lax.broadcasted_iota(jnp.int32, (span, 1), 0) < size
    for h in range(heads_ref.shape[1] // head_width):
        columns = slice(h * head_width, (h + 1) * head_width)
        query = head_norm(queries[:, columns], query_gain_ref[...]).astype(jnp.bfloat16)
        key = head_norm(keys[:, columns], key_gain_ref[...]).astype(jnp.bfloat16)
        scores = lax.dot_general(
            query, key, (((1,), (1,)), ((), ())), preferred_element_type=jnp.float32
        ) * (1.0 / math.sqrt(head_width))
        raised = jnp.where(inside, jnp.exp(scores), 0.0)
        scale = jnp.where(kept, 1.0 / jnp.sum(raised, axis=-1, keepdims=True), 0.0)
        weights = (raised * scale).astype(jnp.bfloat16)
        head = dot32(weights, values[:, columns]).astype(jnp.bfloat16)
        heads_ref[lines, columns] = head
        head_mean = jnp.sum(head.astype(jnp.float32), axis=0, keepdims=True) / count
        means_ref[:, columns] = jnp.where(here, head_mean, means_ref[:, columns])

    @pl.when(k == rows - 1)
    def _():
        heads_ref[rows * span :, :] = means_ref[...].astype(jnp.bfloat16)


def attend(place, counts, plan, qkv, resid, query_gain, key_gain, span, after):
    rows = counts.shape[0]
    local, features = qkv.shape[2], resid.shape[1]
    extra = -(-rows // 16) * 16
    fixed = lambda shape: pl.BlockSpec(shape, lambda k, *_: (0,) * len(shape))
    return pl.pallas_call(
        lambda *refs: attend_kernel(rows, span, *refs),
        grid_spec=pltpu.PrefetchScalarGridSpec(
            num_scalar_prefetch=3,
            grid=(rows,),
            in_specs=[fixed(x.shape) for x in (qkv, resid, query_gain, key_gain)]
            + [pl.BlockSpec(memory_space=pl.ANY)] * len(after),
            out_specs=[
                fixed((rows * span + extra, local)),
                pl.BlockSpec((span, features), lambda k, *_: (k, 0)),
                fixed((extra, features)),
            ],
            scratch_shapes=[pltpu.VMEM((extra, local), jnp.float32)],
        ),
        out_shape=[
            jax.ShapeDtypeStruct((rows * span + extra, local), jnp.bfloat16),
            jax.ShapeDtypeStruct((rows * span, features), jnp.bfloat16),
            jax.ShapeDtypeStruct((extra, features), jnp.float32),
        ],
        compiler_params=pltpu.CompilerParams(vmem_limit_bytes=VMEM_BYTES),
        cost_estimate=pl.CostEstimate(
            flops=10_000_000_000, bytes_accessed=12_000_000, transcendentals=0
        ),
        name="attend",
    )(place, counts, plan, qkv, resid, query_gain, key_gain, *after)


def early_kernel(rows, with_late, place_ref, *refs):
    head_refs = refs[:rows]
    own_ref, *piece_refs = refs[rows : rows + 4]
    resid_ref, means_ref = refs[rows + 4 : rows + 6]
    held_ref, weight_ref, head_sems, weight_sems, late_sem = refs[-5:]
    total_ref, late_ref = refs[-7:-5] if with_late else (refs[-6], None)
    my_row, my_part, my_group = place_ref[0], place_ref[1], place_ref[2]
    tiles, used, tile = weight_ref.shape
    depth = head_refs[0].shape[1]
    half = depth // 2

    def head_copies(act):
        for x in range(rows):
            step = lax.rem(my_row - (x ^ my_part) + rows, rows)
            for s in range(2):
                turned = jnp.where(step == 0, s, s ^ my_group)
                start = pl.multiple_of(step * depth + turned * half, 128)
                copy = pltpu.make_async_copy(
                    head_refs[x].at[: held_ref.shape[0], s * half : (s + 1) * half],
                    held_ref.at[:, pl.ds(start, half)],
                    head_sems.at[x, s],
                )
                act(copy)

    def weight_copies(i, act):
        column = i * tile
        sources = [own_ref.at[:, column : column + tile]]
        sources += [piece_ref.at[:, column : column + tile] for piece_ref in piece_refs]
        starts = [0, depth, depth + half, depth + 2 * half]
        for n, (source, start) in enumerate(zip(sources, starts)):
            act(
                pltpu.make_async_copy(
                    source, weight_ref.at[i, pl.ds(start, source.shape[0])], weight_sems.at[i, n]
                )
            )

    i = pl.program_id(0)

    @pl.when(i == 0)
    def _():
        head_copies(lambda copy: copy.start())
        for j in range(tiles):
            weight_copies(j, lambda copy: copy.start())
        head_copies(lambda copy: copy.wait())
        if with_late:
            pltpu.make_async_copy(held_ref.at[:, used:], late_ref, late_sem).start()

    for j in range(tiles):

        @pl.when(i == j)
        def _():
            weight_copies(j, lambda copy: copy.wait())

    length = resid_ref.shape[0]
    for start in range(0, length, 256):
        added = min(256, length - start)
        last = start + added == length
        lines = slice(start, None if last else start + added)
        total = dot32(held_ref[lines, :used], weight_ref[i])
        lines = slice(start, start + added)
        total_ref[lines] = total[:added] + resid_ref[lines].astype(jnp.float32)
        if last:
            total_ref[length:] = total[added:] + means_ref[...]

    if with_late:

        @pl.when(i == tiles - 1)
        def _():
            pltpu.make_async_copy(held_ref.at[:, used:], late_ref, late_sem).wait()


def project_early(place, heads, own, pieces, resid, means, chunk, with_late, after):
    rows = len(heads)
    length, depth = heads[0].shape
    width = pieces[0].shape[1]
    used = depth * 5 // 2
    tile = 256
    tiles = width // tile
    anywhere = pl.BlockSpec(memory_space=pl.ANY)
    late = [jax.ShapeDtypeStruct((length, rows * depth - used), jnp.bfloat16)] if with_late else []
    return pl.pallas_call(
        lambda place_ref, *refs: early_kernel(
            rows, with_late, place_ref, *refs[: rows + 6], *refs[rows + 6 + len(after) :]
        ),
        grid=(tiles,),
        in_specs=[pl.BlockSpec(memory_space=pltpu.SMEM)]
        + [anywhere] * (rows + 4)
        + [
            pl.BlockSpec((x.shape[0], tile), lambda i: (0, chunk * tiles + i))
            for x in (resid, means)
        ]
        + [anywhere] * len(after),
        out_specs=[pl.BlockSpec((length, tile), lambda i: (0, i))] + [anywhere] * len(late),
        scratch_shapes=[
            pltpu.VMEM((length, rows * depth), jnp.bfloat16),
            pltpu.VMEM((tiles, used, tile), jnp.bfloat16),
            pltpu.SemaphoreType.DMA((rows, 2)),
            pltpu.SemaphoreType.DMA((tiles, 4)),
            pltpu.SemaphoreType.DMA,
        ],
        out_shape=[jax.ShapeDtypeStruct((length, width), jnp.float32)] + late,
        compiler_params=pltpu.CompilerParams(vmem_limit_bytes=VMEM_BYTES),
        cost_estimate=pl.CostEstimate(
            flops=EARLY_FLOPS, bytes_accessed=1000, transcendentals=0
        ),
        name="project_early",
    )(place, *heads, own, *pieces, resid, means, *after)


def late_kernel(rows, total_ref, late_ref, *refs):
    piece_refs, out_refs = refs[:3], refs[-rows:]
    half = piece_refs[0].shape[0]
    span = out_refs[0].shape[0]
    for k in range(rows):
        lines = slice(k * span, (k + 1) * span)
        total = total_ref[lines, :]
        for n in range(3):
            total = total + dot32(late_ref[lines, n * half : (n + 1) * half], piece_refs[n][...])
        out_refs[k][...] = total.astype(jnp.bfloat16)


def pool_kernel(rows, chunks, *refs):
    late_ref, total_refs = refs[0], refs[1 : 1 + chunks]
    piece_refs, pooled_ref = refs[1 + chunks : -1], refs[-1]
    half, width = piece_refs[0].shape
    for c in range(chunks):
        total = total_refs[c][...]
        for n in range(3):
            columns = slice(n * half, (n + 1) * half)
            total = total + dot32(late_ref[:, columns], piece_refs[3 * c + n][...])
        pooled_ref[:, c * width : (c + 1) * width] = total[:rows].astype(jnp.bfloat16)


def project_pooled(totals, late, pieces, rows, start):
    chunks = len(totals)
    extra = late.shape[0] - start
    width = totals[0].shape[1]
    flat = [piece for chunk in pieces for piece in chunk]
    whole = lambda x: pl.BlockSpec(x.shape, lambda i: (0, 0))
    tail = lambda x: pl.BlockSpec((extra, x.shape[1]), lambda i: (start // extra, 0))
    return pl.pallas_call(
        lambda *refs: pool_kernel(rows, chunks, *refs),
        grid=(1,),
        in_specs=[tail(late)] + [tail(x) for x in totals] + [whole(x) for x in flat],
        out_specs=pl.BlockSpec((rows, chunks * width), lambda i: (0, 0)),
        out_shape=jax.ShapeDtypeStruct((rows, chunks * width), jnp.bfloat16),
        compiler_params=pltpu.CompilerParams(vmem_limit_bytes=VMEM_BYTES),
        cost_estimate=pl.CostEstimate(flops=1000, bytes_accessed=1000, transcendentals=0),
        name="project_pooled",
    )(late, *totals, *flat)


def project_late(total, late, pieces, rows, span, after):
    half, width = pieces[0].shape
    length = total.shape[0]
    tile = 256
    tiles = width // tile
    return pl.pallas_call(
        lambda *refs: late_kernel(rows, *refs),
        grid=(tiles,),
        in_specs=[
            pl.BlockSpec((length, tile), lambda i: (0, i)),
            pl.BlockSpec(late.shape, lambda i: (0, 0)),
        ]
        + [pl.BlockSpec((half, tile), lambda i: (0, i))] * 3
        + [pl.BlockSpec(memory_space=pl.ANY)] * len(after),
        out_specs=[pl.BlockSpec((span, tile), lambda i: (0, i))] * rows,
        out_shape=[jax.ShapeDtypeStruct((span, width), jnp.bfloat16)] * rows,
        compiler_params=pltpu.CompilerParams(vmem_limit_bytes=VMEM_BYTES),
        cost_estimate=pl.CostEstimate(
            flops=6 * length * half * width, bytes_accessed=6_000_000, transcendentals=0
        ),
        name="project_late",
    )(total, late, *pieces, *after)


def one_hot(hits):
    return hits.astype(jnp.float32).astype(jnp.bfloat16)


def local_call(kernel, out_shape, operands, after, place, name, flops):
    whole = pl.BlockSpec(memory_space=pltpu.VMEM)
    return pl.pallas_call(
        kernel,
        in_specs=[pl.BlockSpec(memory_space=pltpu.SMEM)]
        + [whole] * len(operands)
        + [pl.BlockSpec(memory_space=pl.ANY)] * len(after),
        out_specs=jax.tree.map(lambda _: whole, out_shape),
        out_shape=out_shape,
        compiler_params=pltpu.CompilerParams(vmem_limit_bytes=VMEM_BYTES),
        cost_estimate=pl.CostEstimate(flops=flops, bytes_accessed=1000, transcendentals=0),
        name=name,
    )(place, *operands, *after)


def after_all(values, after):
    return lax.optimization_barrier((list(values), list(after)))[0]


def terms_kernel(rows, place_ref, *refs):
    pooled_refs = refs[:rows]
    weight_ref = refs[rows]
    out_refs = refs[-rows - 1 : -1]
    pooled_ref = refs[-1]
    count = rows * rows

    @pl.when(pl.program_id(0) == 0)
    def _():
        wanted = lax.broadcasted_iota(jnp.int32, (count, rows), 0)
        image = lax.broadcasted_iota(jnp.int32, (count, rows), 1)
        part = wanted // rows ^ place_ref[1]
        pooled = None
        for k in range(rows):
            row = lax.rem(place_ref[0] - k + rows, rows)
            order = one_hot((wanted % rows == row) & (image == part))
            term = dot32(order, pooled_refs[k][...])
            pooled = term if pooled is None else pooled + term
        pooled_ref[...] = pooled.astype(jnp.bfloat16)

    terms = dot32(pooled_ref[...], weight_ref[...]).astype(jnp.bfloat16)
    for k in range(rows):
        out_refs[k][...] = terms[k * rows : (k + 1) * rows]


def label_terms_by_part(place, pooled, label_weight, after):
    rows = len(pooled)
    features, classes = label_weight.shape
    tile = 512
    return pl.pallas_call(
        lambda *refs: terms_kernel(rows, *refs),
        grid_spec=pltpu.PrefetchScalarGridSpec(
            num_scalar_prefetch=1,
            grid=(classes // tile,),
            in_specs=[pl.BlockSpec(x.shape, lambda i, *_: (0, 0)) for x in pooled]
            + [pl.BlockSpec((features, tile), lambda i, *_: (0, i))]
            + [pl.BlockSpec(memory_space=pl.ANY)] * len(after),
            out_specs=[pl.BlockSpec((rows, tile), lambda i, *_: (0, i))] * rows,
            scratch_shapes=[pltpu.VMEM((rows * rows, features), jnp.bfloat16)],
        ),
        out_shape=[jax.ShapeDtypeStruct((rows, classes), jnp.bfloat16)] * rows,
        compiler_params=pltpu.CompilerParams(vmem_limit_bytes=VMEM_BYTES),
        cost_estimate=pl.CostEstimate(
            flops=2 * rows * rows * features * classes,
            bytes_accessed=12_000_000,
            transcendentals=0,
        ),
        name="label_terms",
    )(place, *pooled, label_weight, *after)


def probs_kernel(rows, place_ref, *refs):
    term_refs = refs[:rows]
    bias_ref = refs[rows]
    out_refs = refs[-rows:]
    logits = term_refs[0][...].astype(jnp.float32)
    for k in range(1, rows):
        logits = logits + term_refs[k][...].astype(jnp.float32)
    probs = jax.nn.sigmoid(logits + bias_ref[...])
    line = lax.broadcasted_iota(jnp.int32, (rows, 1), 0)
    for k in range(rows):
        row = lax.rem(place_ref[0] + k, rows)
        picked = jnp.sum(jnp.where(line == row, probs, 0.0), axis=0, keepdims=True)
        out_refs[k][...] = picked.astype(jnp.bfloat16)


def labels_kernel(rows, place_ref, *refs):
    out_ref = refs[-1]
    classes = refs[0].shape[1]
    for k in range(rows):
        row = lax.rem(place_ref[0] - k + rows, rows)
        columns = pl.ds(pl.multiple_of(row * classes, 128), classes)
        out_ref[:, columns] = refs[k][...].astype(jnp.float32)


def settle_kernel(rows, place_ref, counts_ref, plan_ref, *refs):
    block_refs = refs[:rows]
    out_ref = refs[-1]
    my_row = place_ref[0]
    tokens, span = out_ref.shape[0], block_refs[0].shape[0]
    token = lax.broadcasted_iota(jnp.int32, (tokens, span), 0)
    slot = lax.broadcasted_iota(jnp.int32, (tokens, span), 1)
    sizes = [image_for(counts_ref, plan_ref, r, my_row, rows)[2] for r in range(rows)]
    total = None
    for k in range(rows):
        source = lax.rem(my_row - k + rows, rows)
        start, size = 0, 0
        for r in range(rows):
            start = start + jnp.where(r < source, sizes[r], 0)
            size = jnp.where(r == source, sizes[r], size)
        select = ((token - slot == start) & (slot < size)).astype(jnp.float32).astype(jnp.bfloat16)
        term = dot32(select, block_refs[k][...])
        total = term if total is None else total + term
    out_ref[...] = total.astype(jnp.bfloat16)


def settle(place, counts, plan, blocks, chunk, features, earlier, after):
    rows = len(blocks)
    span, width = blocks[0].shape
    tile = 256
    tiles = width // tile
    first = chunk * tiles
    more = [] if earlier is None else [earlier]
    return pl.pallas_call(
        lambda *refs: settle_kernel(rows, *refs),
        grid_spec=pltpu.PrefetchScalarGridSpec(
            num_scalar_prefetch=3,
            grid=(tiles,),
            in_specs=[pl.BlockSpec((span, tile), lambda i, *_: (0, i))] * rows
            + [pl.BlockSpec(memory_space=pl.ANY)] * (len(more) + len(after)),
            out_specs=pl.BlockSpec((TOK, tile), lambda i, *_: (0, first + i)),
        ),
        out_shape=jax.ShapeDtypeStruct((TOK, features), jnp.bfloat16),
        input_output_aliases={3 + rows: 0} if more else {},
        compiler_params=pltpu.CompilerParams(vmem_limit_bytes=VMEM_BYTES),
        cost_estimate=pl.CostEstimate(
            flops=2 * TOK * rows * span * width, bytes_accessed=2_000_000, transcendentals=0
        ),
        name="settle",
    )(place, counts, plan, *blocks, *more, *after)


def on_device_rings(
    qkv_home,
    resid_home,
    out_weight,
    label_weight,
    label_bias,
    query_gain,
    key_gain,
    patch_counts,
    move_plan,
    segment_ids,
):
    rows = lax.axis_size("dp")
    parts = lax.axis_size("mp")
    sharers = lax.axis_size("groups")
    my_row = lax.axis_index("dp")
    my_part = lax.axis_index("mp")
    my_group = lax.axis_index("groups")
    slots = segment_ids.shape[1]
    span = -(-(slots // rows) // 16) * 16
    padded = -(-slots // 16) * 16 + span
    depth, features = out_weight.shape
    half = depth // sharers
    width = features // CHUNKS
    place = jnp.stack([my_row, my_part, my_group]).astype(jnp.int32)

    mine = lax.dynamic_slice_in_dim(out_weight, my_group * half, half, 0)
    moving = [mine[:, c * width : (c + 1) * width] for c in range(CHUNKS)]
    moving = [send(x, "dp", shifted(rows, 1), f"w{c}_1") for c, x in enumerate(moving)]

    qkv = jnp.pad(jnp.transpose(qkv_home[0], (1, 0, 2)), ((0, 0), (0, padded - slots), (0, 0)))
    heads, resid, resid_means = attend(
        place,
        patch_counts,
        move_plan,
        qkv,
        jnp.pad(resid_home[0], ((0, padded - slots), (0, 0))),
        query_gain[None],
        key_gain[None],
        span,
        [],
    )
    heads = after_all([heads], moving)[0]
    across = send(heads, "mp", crossed(parts, 2), "h_2")
    beside = send(heads, "mp", crossed(parts, 1), "h_1")

    following = [send(x, "dp", shifted(rows, 1), f"w{c}_2") for c, x in enumerate(moving)]
    others = [
        send(x, "groups", crossed(sharers, 1), f"y{c}_1") for c, x in enumerate(moving)
    ]
    pieces = [[x, y, z] for x, y, z in zip(moving, others, following)]
    turned = after_all([across], [*following, *others])[0]
    beyond = send(turned, "mp", crossed(parts, 1), "h_3")
    every_head = [heads, beside, across, beyond]

    totals, late, early, moving = [], None, pieces, following
    pieces = []
    for c in range(CHUNKS):
        after = totals
        x = after_all([moving[c]], after)[0] if c else moving[c]
        x = send(x, "dp", shifted(rows, 1), f"w{c}_3")
        total, *more = project_early(
            place,
            every_head,
            out_weight[:, c * width : (c + 1) * width],
            early[c],
            resid,
            resid_means,
            c,
            c == 0,
            [totals[0], pieces[0][1]] if c else [],
        )
        totals.append(total)
        late = more[0] if more else late
        y = after_all([moving[c]], [x, total, pieces[0][2]])[0] if c else moving[c]
        y = send(y, "groups", crossed(sharers, 1), f"y{c}_2")
        z = after_all([x], [total] if c else [total, y])[0]
        z = send(z, "groups", crossed(sharers, 1), f"y{c}_3")
        pieces.append([y, x, z])

    arrived = []
    for c in range(CHUNKS):
        if c == CHUNKS - 1:
            pooled = project_pooled(totals, late, pieces, rows, rows * span)
            pooled = [pooled] + [
                send(pooled, "dp", shifted(rows, k), f"p_{k}") for k in range(1, rows)
            ]
        blocks = project_late(
            totals[c], late, pieces[c], rows, span, arrived[0][1:] if c else []
        )
        if c == CHUNKS - 1:
            blocks = after_all(blocks, pooled[1:])
        arrived.append(
            [blocks[0]] + [send(blocks[k], "dp", shifted(rows, k), f"m{c}_{k}") for k in range(1, rows)]
        )

    classes = label_weight.shape[1]
    terms = label_terms_by_part(place, pooled, label_weight, [])
    terms = [terms[0]] + [
        send(terms[k], "mp", crossed(parts, k), f"t_{k}") for k in range(1, parts)
    ]
    probs = local_call(
        lambda *refs: probs_kernel(rows, *refs),
        [jax.ShapeDtypeStruct((1, classes), jnp.bfloat16)] * rows,
        [*terms, label_bias[None]],
        [],
        place,
        "probs",
        1000,
    )
    probs = [probs[0]] + [send(probs[k], "dp", shifted(rows, k), f"l_{k}") for k in range(1, rows)]
    labels = local_call(
        lambda *refs: labels_kernel(rows, *refs),
        jax.ShapeDtypeStruct((1, rows * classes), jnp.float32),
        probs,
        [],
        place,
        "labels",
        1000,
    )
    mixed = None
    for c in range(CHUNKS):
        mixed = settle(place, patch_counts, move_plan, arrived[c], c, features, mixed, [])
    labels = labels[None]
    return (mixed[None], labels)

def attend_home(qkv_rows, seg_rows, query_gain, key_gain):
    length = qkv_rows.shape[0]
    head_width = query_gain.shape[0]
    head_count = qkv_rows.shape[2] // head_width
    split_parts = qkv_rows.reshape(length, 3, head_count, head_width)
    queries = head_norm(split_parts[:, 0].astype(jnp.float32), query_gain).astype(jnp.bfloat16)
    key_rows = head_norm(split_parts[:, 1].astype(jnp.float32), key_gain).astype(jnp.bfloat16)
    scores = jnp.einsum(
        "qhd,khd->hqk", queries, key_rows, preferred_element_type=jnp.float32
    ) / math.sqrt(head_width)
    same_image = seg_rows[:, None] == seg_rows[None, :]
    raised = jnp.where(same_image[None], jnp.exp(scores), 0.0)
    weights = (raised / jnp.sum(raised, axis=-1, keepdims=True)).astype(jnp.bfloat16)
    head_out = jnp.einsum(
        "hqk,khd->qhd", weights, split_parts[:, 2], preferred_element_type=jnp.float32
    )
    return head_out.reshape(length, head_count * head_width).astype(jnp.bfloat16)


def project_home(heads_local, resid_rows, out_weight):
    gathered = lax.all_gather(heads_local, "mp", axis=1, tiled=True)
    running = resid_rows.astype(jnp.float32) + jnp.dot(
        gathered,
        lax.all_gather(out_weight, "dp", axis=0, tiled=True),
        preferred_element_type=jnp.float32,
    )
    return running.astype(jnp.bfloat16)


def pool(row_mixed, seg_rows, count_row):
    images = count_row.shape[0]
    member_ids = lax.broadcasted_iota(jnp.int32, (images, seg_rows.shape[0]), 0)
    member = (member_ids == seg_rows[None, :]).astype(jnp.bfloat16)
    image_sums = jnp.dot(member, row_mixed, preferred_element_type=jnp.float32)
    return (image_sums / count_row[:, None].astype(jnp.float32)).astype(jnp.bfloat16)


def label_terms(pooled, label_weight):
    return jnp.einsum(
        "abd,dc->abc",
        lax.all_gather(pooled[None], "dp", axis=0, tiled=True),
        label_weight,
        preferred_element_type=jnp.float32,
    )


def pick(values, row_index, is_valid):
    taken = jnp.take(values, row_index, axis=0)
    taken = taken.reshape(is_valid.shape + values.shape[1:])
    keep_mask = is_valid.reshape(is_valid.shape + (1,) * (values.ndim - 1))
    return jnp.where(keep_mask, taken, jnp.zeros_like(taken))


def on_device(
    qkv_home,
    resid_home,
    out_weight,
    label_weight,
    label_bias,
    query_gain,
    key_gain,
    patch_counts,
    move_plan,
    segment_ids,
):
    row_count = lax.axis_size("dp")
    my_index = lax.axis_index("dp")
    home_slots = segment_ids.shape[1]
    pair_slots = home_slots // row_count
    image_ids = lax.broadcasted_iota(jnp.int32, (row_count, row_count, row_count), 2)
    image_ends = jnp.cumsum(patch_counts, axis=1)
    starts = image_ends - patch_counts
    matches = (move_plan[:, :, None] == image_ids).astype(jnp.int32)
    image_sizes = jnp.sum(patch_counts[:, :, None] * matches, axis=1)
    firsts = jnp.sum(starts[:, :, None] * matches, axis=1)
    send_sizes = lax.dynamic_index_in_dim(image_sizes, my_index, 0, keepdims=False)
    send_firsts = lax.dynamic_index_in_dim(firsts, my_index, 0, keepdims=False)
    within = lax.broadcasted_iota(jnp.int32, (row_count, pair_slots), 1)
    send_valid = within < send_sizes[:, None]
    send_index = jnp.minimum(send_firsts[:, None] + within, home_slots - 1).reshape(-1)
    arrive_sizes = lax.dynamic_index_in_dim(image_sizes, my_index, 1, keepdims=False)
    arrive_ends = jnp.cumsum(arrive_sizes)
    arrive_starts = arrive_ends - arrive_sizes
    slot_grid = lax.broadcasted_iota(jnp.int32, (TOK, row_count), 0)
    source = jnp.sum((slot_grid >= arrive_ends[None, :]).astype(jnp.int32), axis=1)
    chosen = (source[:, None] == lax.broadcasted_iota(jnp.int32, (TOK, row_count), 1)).astype(
        jnp.int32
    )
    arrive_index = (
        source * pair_slots + slot_grid[:, 0] - jnp.sum(chosen * arrive_starts[None, :], axis=1)
    )
    home_mixed = project_home(
        attend_home(qkv_home[0], segment_ids[0], query_gain, key_gain), resid_home[0], out_weight
    )
    count_row = lax.dynamic_index_in_dim(patch_counts, my_index, 0, keepdims=False)
    pooled = pool(home_mixed, segment_ids[0], count_row)
    partial_value = label_terms(pooled, label_weight)
    send_mixed = pick(home_mixed, send_index, send_valid)
    got_mixed = lax.all_to_all(send_mixed, "dp", split_axis=0, concat_axis=0, tiled=True)
    mixed = jnp.take(got_mixed.reshape(row_count * pair_slots, -1), arrive_index, axis=0)
    logit_sums = lax.psum_scatter(
        partial_value.astype(jnp.bfloat16), "mp", scatter_dimension=1, tiled=True
    ).astype(jnp.float32)
    class_probs = jax.nn.sigmoid(logit_sums + label_bias[None, None, :])
    labels = lax.all_to_all(
        class_probs.astype(jnp.bfloat16), "dp", split_axis=0, concat_axis=2, tiled=True
    ).astype(class_probs.dtype)
    return (mixed[None], labels)

def solution(mesh):
    rows, parts, sharers = (mesh.shape[name] for name in ("dp", "mp", "groups"))
    small = rows == parts == 4 and sharers == 2
    return jax.shard_map(
        on_device_rings if small else on_device,
        mesh=mesh,
        in_specs=(
            P(("groups", "dp"), None, None, "mp"),
            P(("groups", "dp"), None, "mp"),
            P("dp", "mp"),
            P("mp", "dp"),
            P("dp"),
            P(),
            P(),
            P("groups", None),
            P("groups", None),
            P(("groups", "dp"), None),
        ),
        out_specs=(P(("groups", "dp"), None, "mp"), P(("groups", "dp"), "mp", None)),
        check_vma=False,
    )
```

```python
import math

import jax
import jax.numpy as jnp
from jax import lax
from jax.experimental import pallas as pl
from jax.experimental.pallas import tpu as pltpu
from jax.sharding import PartitionSpec as P

TOK = 384
CHUNKS = 2
VMEM_BYTES = 24 * 1024 * 1024
EARLY_FLOPS = 4_000_000_000


EPSILON = 1e-06


def head_norm(values, norm_gain):
    center = values - jnp.mean(values, axis=-1, keepdims=True)
    spread = jnp.mean(center * center, axis=-1, keepdims=True)
    return center * lax.rsqrt(spread + EPSILON) * norm_gain


def shifted(count, by):
    return [(i, (i + by) % count) for i in range(count)]


def crossed(count, by):
    return [(i, i ^ by) for i in range(count)]


def send(values, axis, pairs, name):
    with jax.named_scope(name):
        return lax.ppermute(values, axis, pairs)


def dot32(left, right):
    return jnp.dot(left, right, preferred_element_type=jnp.float32)


def at(values, index, axis=0):
    return lax.dynamic_index_in_dim(values, index, axis, keepdims=False)


def image_for(counts_ref, plan_ref, row, dest, images):
    image, first, size, before = 0, 0, 0, 0
    for j in range(images):
        count = counts_ref[row, j]
        hit = plan_ref[row, j] == dest
        image = jnp.where(hit, j, image)
        first = jnp.where(hit, before, first)
        size = jnp.where(hit, count, size)
        before = before + count
    return image, first, size


def attend_kernel(
    rows,
    span,
    place_ref,
    counts_ref,
    plan_ref,
    qkv_ref,
    resid_ref,
    query_gain_ref,
    key_gain_ref,
    *rest,
):
    heads_ref, sent_ref, resid_means_ref, means_ref = rest[-4:]
    k = pl.program_id(0)
    lines = pl.ds(pl.multiple_of(k * span, 16), span)
    my_row = place_ref[0]
    image, first, size = image_for(
        counts_ref, plan_ref, my_row, lax.rem(my_row + k, rows), rows
    )
    window = span + 16
    begin = pl.multiple_of(first // 16 * 16, 16)
    shift = first - begin
    taken = lax.broadcasted_iota(jnp.int32, (span, window), 0)
    slot = lax.broadcasted_iota(jnp.int32, (span, window), 1)
    select = ((slot - taken == shift) & (taken < size)).astype(jnp.float32).astype(jnp.bfloat16)
    count = size.astype(jnp.float32)
    resid = dot32(select, resid_ref[pl.ds(begin, window), :])
    sent_ref[...] = resid.astype(jnp.bfloat16)
    here = lax.broadcasted_iota(jnp.int32, (means_ref.shape[0], 1), 0) == image
    resid_mean = jnp.sum(resid, axis=0, keepdims=True) / count
    resid_means_ref[...] = jnp.where(here, resid_mean, resid_means_ref[...])

    @pl.when(k == 0)
    def _():
        means_ref[...] = jnp.zeros_like(means_ref)
    queries = dot32(select, qkv_ref[0, pl.ds(begin, window), :])
    keys = dot32(select, qkv_ref[1, pl.ds(begin, window), :])
    values = dot32(select, qkv_ref[2, pl.ds(begin, window), :]).astype(jnp.bfloat16)
    head_width = query_gain_ref.shape[1]
    inside = lax.broadcasted_iota(jnp.int32, (span, span), 1) < size
    kept = lax.broadcasted_iota(jnp.int32, (span, 1), 0) < size
    for h in range(heads_ref.shape[1] // head_width):
        columns = slice(h * head_width, (h + 1) * head_width)
        query = head_norm(queries[:, columns], query_gain_ref[...]).astype(jnp.bfloat16)
        key = head_norm(keys[:, columns], key_gain_ref[...]).astype(jnp.bfloat16)
        scores = lax.dot_general(
            query, key, (((1,), (1,)), ((), ())), preferred_element_type=jnp.float32
        ) * (1.0 / math.sqrt(head_width))
        raised = jnp.where(inside, jnp.exp(scores), 0.0)
        scale = jnp.where(kept, 1.0 / jnp.sum(raised, axis=-1, keepdims=True), 0.0)
        weights = (raised * scale).astype(jnp.bfloat16)
        head = dot32(weights, values[:, columns]).astype(jnp.bfloat16)
        heads_ref[lines, columns] = head
        head_mean = jnp.sum(head.astype(jnp.float32), axis=0, keepdims=True) / count
        means_ref[:, columns] = jnp.where(here, head_mean, means_ref[:, columns])

    @pl.when(k == rows - 1)
    def _():
        heads_ref[rows * span :, :] = means_ref[...].astype(jnp.bfloat16)


def attend(place, counts, plan, qkv, resid, query_gain, key_gain, span, after):
    rows = counts.shape[0]
    local, features = qkv.shape[2], resid.shape[1]
    extra = -(-rows // 16) * 16
    fixed = lambda shape: pl.BlockSpec(shape, lambda k, *_: (0,) * len(shape))
    return pl.pallas_call(
        lambda *refs: attend_kernel(rows, span, *refs),
        grid_spec=pltpu.PrefetchScalarGridSpec(
            num_scalar_prefetch=3,
            grid=(rows,),
            in_specs=[fixed(x.shape) for x in (qkv, resid, query_gain, key_gain)]
            + [pl.BlockSpec(memory_space=pl.ANY)] * len(after),
            out_specs=[
                fixed((rows * span + extra, local)),
                pl.BlockSpec((span, features), lambda k, *_: (k, 0)),
                fixed((extra, features)),
            ],
            scratch_shapes=[pltpu.VMEM((extra, local), jnp.float32)],
        ),
        out_shape=[
            jax.ShapeDtypeStruct((rows * span + extra, local), jnp.bfloat16),
            jax.ShapeDtypeStruct((rows * span, features), jnp.bfloat16),
            jax.ShapeDtypeStruct((extra, features), jnp.float32),
        ],
        compiler_params=pltpu.CompilerParams(vmem_limit_bytes=VMEM_BYTES),
        cost_estimate=pl.CostEstimate(
            flops=10_000_000_000, bytes_accessed=12_000_000, transcendentals=0
        ),
        name="attend",
    )(place, counts, plan, qkv, resid, query_gain, key_gain, *after)


def early_kernel(rows, with_late, place_ref, *refs):
    head_refs = refs[:rows]
    own_ref, *piece_refs = refs[rows : rows + 4]
    resid_ref, means_ref = refs[rows + 4 : rows + 6]
    held_ref, weight_ref, head_sems, weight_sems, late_sem = refs[-5:]
    total_ref, late_ref = refs[-7:-5] if with_late else (refs[-6], None)
    my_row, my_part, my_group = place_ref[0], place_ref[1], place_ref[2]
    tiles, used, tile = weight_ref.shape
    depth = head_refs[0].shape[1]
    half = depth // 2

    def head_copies(act):
        for x in range(rows):
            step = lax.rem(my_row - (x ^ my_part) + rows, rows)
            for s in range(2):
                turned = jnp.where(step == 0, s, s ^ my_group)
                start = pl.multiple_of(step * depth + turned * half, 128)
                copy = pltpu.make_async_copy(
                    head_refs[x].at[: held_ref.shape[0], s * half : (s + 1) * half],
                    held_ref.at[:, pl.ds(start, half)],
                    head_sems.at[x, s],
                )
                act(copy)

    def weight_copies(i, act):
        column = i * tile
        sources = [own_ref.at[:, column : column + tile]]
        sources += [piece_ref.at[:, column : column + tile] for piece_ref in piece_refs]
        starts = [0, depth, depth + half, depth + 2 * half]
        for n, (source, start) in enumerate(zip(sources, starts)):
            act(
                pltpu.make_async_copy(
                    source, weight_ref.at[i, pl.ds(start, source.shape[0])], weight_sems.at[i, n]
                )
            )

    i = pl.program_id(0)

    @pl.when(i == 0)
    def _():
        head_copies(lambda copy: copy.start())
        for j in range(tiles):
            weight_copies(j, lambda copy: copy.start())
        head_copies(lambda copy: copy.wait())
        if with_late:
            pltpu.make_async_copy(held_ref.at[:, used:], late_ref, late_sem).start()

    for j in range(tiles):

        @pl.when(i == j)
        def _():
            weight_copies(j, lambda copy: copy.wait())

    length = resid_ref.shape[0]
    for start in range(0, length, 256):
        added = min(256, length - start)
        last = start + added == length
        lines = slice(start, None if last else start + added)
        total = dot32(held_ref[lines, :used], weight_ref[i])
        lines = slice(start, start + added)
        total_ref[lines] = total[:added] + resid_ref[lines].astype(jnp.float32)
        if last:
            total_ref[length:] = total[added:] + means_ref[...]

    if with_late:

        @pl.when(i == tiles - 1)
        def _():
            pltpu.make_async_copy(held_ref.at[:, used:], late_ref, late_sem).wait()


def project_early(place, heads, own, pieces, resid, means, chunk, with_late, after):
    rows = len(heads)
    length, depth = heads[0].shape
    width = pieces[0].shape[1]
    used = depth * 5 // 2
    tile = 256
    tiles = width // tile
    anywhere = pl.BlockSpec(memory_space=pl.ANY)
    late = [jax.ShapeDtypeStruct((length, rows * depth - used), jnp.bfloat16)] if with_late else []
    return pl.pallas_call(
        lambda place_ref, *refs: early_kernel(
            rows, with_late, place_ref, *refs[: rows + 6], *refs[rows + 6 + len(after) :]
        ),
        grid=(tiles,),
        in_specs=[pl.BlockSpec(memory_space=pltpu.SMEM)]
        + [anywhere] * (rows + 4)
        + [
            pl.BlockSpec((x.shape[0], tile), lambda i: (0, chunk * tiles + i))
            for x in (resid, means)
        ]
        + [anywhere] * len(after),
        out_specs=[pl.BlockSpec((length, tile), lambda i: (0, i))] + [anywhere] * len(late),
        scratch_shapes=[
            pltpu.VMEM((length, rows * depth), jnp.bfloat16),
            pltpu.VMEM((tiles, used, tile), jnp.bfloat16),
            pltpu.SemaphoreType.DMA((rows, 2)),
            pltpu.SemaphoreType.DMA((tiles, 4)),
            pltpu.SemaphoreType.DMA,
        ],
        out_shape=[jax.ShapeDtypeStruct((length, width), jnp.float32)] + late,
        compiler_params=pltpu.CompilerParams(vmem_limit_bytes=VMEM_BYTES),
        cost_estimate=pl.CostEstimate(
            flops=EARLY_FLOPS, bytes_accessed=1000, transcendentals=0
        ),
        name="project_early",
    )(place, *heads, own, *pieces, resid, means, *after)


def late_kernel(rows, total_ref, late_ref, *refs):
    piece_refs, out_refs = refs[:3], refs[-rows:]
    half = piece_refs[0].shape[0]
    span = out_refs[0].shape[0]
    for k in range(rows):
        lines = slice(k * span, (k + 1) * span)
        total = total_ref[lines, :]
        for n in range(3):
            total = total + dot32(late_ref[lines, n * half : (n + 1) * half], piece_refs[n][...])
        out_refs[k][...] = total.astype(jnp.bfloat16)


def pool_kernel(rows, chunks, *refs):
    late_ref, total_refs = refs[0], refs[1 : 1 + chunks]
    piece_refs, pooled_ref = refs[1 + chunks : -1], refs[-1]
    half, width = piece_refs[0].shape
    for c in range(chunks):
        total = total_refs[c][...]
        for n in range(3):
            columns = slice(n * half, (n + 1) * half)
            total = total + dot32(late_ref[:, columns], piece_refs[3 * c + n][...])
        pooled_ref[:, c * width : (c + 1) * width] = total[:rows].astype(jnp.bfloat16)


def project_pooled(totals, late, pieces, rows, start):
    chunks = len(totals)
    extra = late.shape[0] - start
    width = totals[0].shape[1]
    flat = [piece for chunk in pieces for piece in chunk]
    whole = lambda x: pl.BlockSpec(x.shape, lambda i: (0, 0))
    tail = lambda x: pl.BlockSpec((extra, x.shape[1]), lambda i: (start // extra, 0))
    return pl.pallas_call(
        lambda *refs: pool_kernel(rows, chunks, *refs),
        grid=(1,),
        in_specs=[tail(late)] + [tail(x) for x in totals] + [whole(x) for x in flat],
        out_specs=pl.BlockSpec((rows, chunks * width), lambda i: (0, 0)),
        out_shape=jax.ShapeDtypeStruct((rows, chunks * width), jnp.bfloat16),
        compiler_params=pltpu.CompilerParams(vmem_limit_bytes=VMEM_BYTES),
        cost_estimate=pl.CostEstimate(flops=1000, bytes_accessed=1000, transcendentals=0),
        name="project_pooled",
    )(late, *totals, *flat)


def project_late(total, late, pieces, rows, span, after):
    half, width = pieces[0].shape
    length = total.shape[0]
    tile = 256
    tiles = width // tile
    return pl.pallas_call(
        lambda *refs: late_kernel(rows, *refs),
        grid=(tiles,),
        in_specs=[
            pl.BlockSpec((length, tile), lambda i: (0, i)),
            pl.BlockSpec(late.shape, lambda i: (0, 0)),
        ]
        + [pl.BlockSpec((half, tile), lambda i: (0, i))] * 3
        + [pl.BlockSpec(memory_space=pl.ANY)] * len(after),
        out_specs=[pl.BlockSpec((span, tile), lambda i: (0, i))] * rows,
        out_shape=[jax.ShapeDtypeStruct((span, width), jnp.bfloat16)] * rows,
        compiler_params=pltpu.CompilerParams(vmem_limit_bytes=VMEM_BYTES),
        cost_estimate=pl.CostEstimate(
            flops=6 * length * half * width, bytes_accessed=6_000_000, transcendentals=0
        ),
        name="project_late",
    )(total, late, *pieces, *after)


def one_hot(hits):
    return hits.astype(jnp.float32).astype(jnp.bfloat16)


def local_call(kernel, out_shape, operands, after, place, name, flops):
    whole = pl.BlockSpec(memory_space=pltpu.VMEM)
    return pl.pallas_call(
        kernel,
        in_specs=[pl.BlockSpec(memory_space=pltpu.SMEM)]
        + [whole] * len(operands)
        + [pl.BlockSpec(memory_space=pl.ANY)] * len(after),
        out_specs=jax.tree.map(lambda _: whole, out_shape),
        out_shape=out_shape,
        compiler_params=pltpu.CompilerParams(vmem_limit_bytes=VMEM_BYTES),
        cost_estimate=pl.CostEstimate(flops=flops, bytes_accessed=1000, transcendentals=0),
        name=name,
    )(place, *operands, *after)


def after_all(values, after):
    return lax.optimization_barrier((list(values), list(after)))[0]


def terms_kernel(rows, place_ref, *refs):
    pooled_refs = refs[:rows]
    weight_ref = refs[rows]
    out_refs = refs[-rows - 1 : -1]
    pooled_ref = refs[-1]
    count = rows * rows

    @pl.when(pl.program_id(0) == 0)
    def _():
        wanted = lax.broadcasted_iota(jnp.int32, (count, rows), 0)
        image = lax.broadcasted_iota(jnp.int32, (count, rows), 1)
        part = wanted // rows ^ place_ref[1]
        pooled = None
        for k in range(rows):
            row = lax.rem(place_ref[0] - k + rows, rows)
            order = one_hot((wanted % rows == row) & (image == part))
            term = dot32(order, pooled_refs[k][...])
            pooled = term if pooled is None else pooled + term
        pooled_ref[...] = pooled.astype(jnp.bfloat16)

    terms = dot32(pooled_ref[...], weight_ref[...]).astype(jnp.bfloat16)
    for k in range(rows):
        out_refs[k][...] = terms[k * rows : (k + 1) * rows]


def label_terms_by_part(place, pooled, label_weight, after):
    rows = len(pooled)
    features, classes = label_weight.shape
    tile = 512
    return pl.pallas_call(
        lambda *refs: terms_kernel(rows, *refs),
        grid_spec=pltpu.PrefetchScalarGridSpec(
            num_scalar_prefetch=1,
            grid=(classes // tile,),
            in_specs=[pl.BlockSpec(x.shape, lambda i, *_: (0, 0)) for x in pooled]
            + [pl.BlockSpec((features, tile), lambda i, *_: (0, i))]
            + [pl.BlockSpec(memory_space=pl.ANY)] * len(after),
            out_specs=[pl.BlockSpec((rows, tile), lambda i, *_: (0, i))] * rows,
            scratch_shapes=[pltpu.VMEM((rows * rows, features), jnp.bfloat16)],
        ),
        out_shape=[jax.ShapeDtypeStruct((rows, classes), jnp.bfloat16)] * rows,
        compiler_params=pltpu.CompilerParams(vmem_limit_bytes=VMEM_BYTES),
        cost_estimate=pl.CostEstimate(
            flops=2 * rows * rows * features * classes,
            bytes_accessed=12_000_000,
            transcendentals=0,
        ),
        name="label_terms",
    )(place, *pooled, label_weight, *after)


def probs_kernel(rows, place_ref, *refs):
    term_refs = refs[:rows]
    bias_ref = refs[rows]
    out_refs = refs[-rows:]
    logits = term_refs[0][...].astype(jnp.float32)
    for k in range(1, rows):
        logits = logits + term_refs[k][...].astype(jnp.float32)
    probs = jax.nn.sigmoid(logits + bias_ref[...])
    line = lax.broadcasted_iota(jnp.int32, (rows, 1), 0)
    for k in range(rows):
        row = lax.rem(place_ref[0] + k, rows)
        picked = jnp.sum(jnp.where(line == row, probs, 0.0), axis=0, keepdims=True)
        out_refs[k][...] = picked.astype(jnp.bfloat16)


def labels_kernel(rows, place_ref, *refs):
    out_ref = refs[-1]
    classes = refs[0].shape[1]
    for k in range(rows):
        row = lax.rem(place_ref[0] - k + rows, rows)
        columns = pl.ds(pl.multiple_of(row * classes, 128), classes)
        out_ref[:, columns] = refs[k][...].astype(jnp.float32)


def settle_kernel(rows, place_ref, counts_ref, plan_ref, *refs):
    block_refs = refs[:rows]
    out_ref = refs[-1]
    my_row = place_ref[0]
    tokens, span = out_ref.shape[0], block_refs[0].shape[0]
    token = lax.broadcasted_iota(jnp.int32, (tokens, span), 0)
    slot = lax.broadcasted_iota(jnp.int32, (tokens, span), 1)
    sizes = [image_for(counts_ref, plan_ref, r, my_row, rows)[2] for r in range(rows)]
    total = None
    for k in range(rows):
        source = lax.rem(my_row - k + rows, rows)
        start, size = 0, 0
        for r in range(rows):
            start = start + jnp.where(r < source, sizes[r], 0)
            size = jnp.where(r == source, sizes[r], size)
        select = ((token - slot == start) & (slot < size)).astype(jnp.float32).astype(jnp.bfloat16)
        term = dot32(select, block_refs[k][...])
        total = term if total is None else total + term
    out_ref[...] = total.astype(jnp.bfloat16)


def settle(place, counts, plan, blocks, chunk, features, earlier, after):
    rows = len(blocks)
    span, width = blocks[0].shape
    tile = 256
    tiles = width // tile
    first = chunk * tiles
    more = [] if earlier is None else [earlier]
    return pl.pallas_call(
        lambda *refs: settle_kernel(rows, *refs),
        grid_spec=pltpu.PrefetchScalarGridSpec(
            num_scalar_prefetch=3,
            grid=(tiles,),
            in_specs=[pl.BlockSpec((span, tile), lambda i, *_: (0, i))] * rows
            + [pl.BlockSpec(memory_space=pl.ANY)] * (len(more) + len(after)),
            out_specs=pl.BlockSpec((TOK, tile), lambda i, *_: (0, first + i)),
        ),
        out_shape=jax.ShapeDtypeStruct((TOK, features), jnp.bfloat16),
        input_output_aliases={3 + rows: 0} if more else {},
        compiler_params=pltpu.CompilerParams(vmem_limit_bytes=VMEM_BYTES),
        cost_estimate=pl.CostEstimate(
            flops=2 * TOK * rows * span * width, bytes_accessed=2_000_000, transcendentals=0
        ),
        name="settle",
    )(place, counts, plan, *blocks, *more, *after)


def on_device_rings(
    qkv_home,
    resid_home,
    out_weight,
    label_weight,
    label_bias,
    query_gain,
    key_gain,
    patch_counts,
    move_plan,
    segment_ids,
):
    rows = lax.axis_size("dp")
    parts = lax.axis_size("mp")
    sharers = lax.axis_size("groups")
    my_row = lax.axis_index("dp")
    my_part = lax.axis_index("mp")
    my_group = lax.axis_index("groups")
    slots = segment_ids.shape[1]
    span = -(-(slots // rows) // 16) * 16
    padded = -(-slots // 16) * 16 + span
    depth, features = out_weight.shape
    half = depth // sharers
    width = features // CHUNKS
    place = jnp.stack([my_row, my_part, my_group]).astype(jnp.int32)

    mine = lax.dynamic_slice_in_dim(out_weight, my_group * half, half, 0)
    moving = [mine[:, c * width : (c + 1) * width] for c in range(CHUNKS)]
    moving = [send(x, "dp", shifted(rows, 1), f"w{c}_1") for c, x in enumerate(moving)]

    qkv = jnp.pad(jnp.transpose(qkv_home[0], (1, 0, 2)), ((0, 0), (0, padded - slots), (0, 0)))
    heads, resid, resid_means = attend(
        place,
        patch_counts,
        move_plan,
        qkv,
        jnp.pad(resid_home[0], ((0, padded - slots), (0, 0))),
        query_gain[None],
        key_gain[None],
        span,
        [],
    )
    heads = after_all([heads], moving)[0]
    across = send(heads, "mp", crossed(parts, 2), "h_2")
    beside = send(heads, "mp", crossed(parts, 1), "h_1")

    following = [send(x, "dp", shifted(rows, 1), f"w{c}_2") for c, x in enumerate(moving)]
    others = [
        send(x, "groups", crossed(sharers, 1), f"y{c}_1") for c, x in enumerate(moving)
    ]
    pieces = [[x, y, z] for x, y, z in zip(moving, others, following)]
    turned = after_all([across], [*following, *others])[0]
    beyond = send(turned, "mp", crossed(parts, 1), "h_3")
    every_head = [heads, beside, across, beyond]

    totals, late, early, moving = [], None, pieces, following
    pieces = []
    for c in range(CHUNKS):
        after = totals
        x = after_all([moving[c]], after)[0] if c else moving[c]
        x = send(x, "dp", shifted(rows, 1), f"w{c}_3")
        total, *more = project_early(
            place,
            every_head,
            out_weight[:, c * width : (c + 1) * width],
            early[c],
            resid,
            resid_means,
            c,
            c == 0,
            [totals[0], pieces[0][1]] if c else [],
        )
        totals.append(total)
        late = more[0] if more else late
        y = after_all([moving[c]], [x, total, pieces[0][2]])[0] if c else moving[c]
        y = send(y, "groups", crossed(sharers, 1), f"y{c}_2")
        z = after_all([x], [total] if c else [total, y])[0]
        z = send(z, "groups", crossed(sharers, 1), f"y{c}_3")
        pieces.append([y, x, z])

    arrived = []
    for c in range(CHUNKS):
        if c == CHUNKS - 1:
            pooled = project_pooled(totals, late, pieces, rows, rows * span)
            pooled = [pooled] + [
                send(pooled, "dp", shifted(rows, k), f"p_{k}") for k in range(1, rows)
            ]
        blocks = project_late(
            totals[c], late, pieces[c], rows, span, arrived[0][1:] if c else []
        )
        if c == CHUNKS - 1:
            blocks = after_all(blocks, pooled[1:])
        arrived.append(
            [blocks[0]] + [send(blocks[k], "dp", shifted(rows, k), f"m{c}_{k}") for k in range(1, rows)]
        )

    classes = label_weight.shape[1]
    terms = label_terms_by_part(place, pooled, label_weight, [])
    terms = [terms[0]] + [
        send(terms[k], "mp", crossed(parts, k), f"t_{k}") for k in range(1, parts)
    ]
    probs = local_call(
        lambda *refs: probs_kernel(rows, *refs),
        [jax.ShapeDtypeStruct((1, classes), jnp.bfloat16)] * rows,
        [*terms, label_bias[None]],
        [],
        place,
        "probs",
        1000,
    )
    probs = [probs[0]] + [send(probs[k], "dp", shifted(rows, k), f"l_{k}") for k in range(1, rows)]
    mixed = None
    for c in range(CHUNKS):
        mixed = settle(place, patch_counts, move_plan, arrived[c], c, features, mixed, [])
    labels = local_call(
        lambda *refs: labels_kernel(rows, *refs),
        jax.ShapeDtypeStruct((1, rows * classes), jnp.float32),
        after_all(probs, [mixed]),
        [],
        place,
        "labels",
        1000,
    )
    labels = labels[None]
    return (mixed[None], labels)

def attend_home(qkv_rows, seg_rows, query_gain, key_gain):
    length = qkv_rows.shape[0]
    head_width = query_gain.shape[0]
    head_count = qkv_rows.shape[2] // head_width
    split_parts = qkv_rows.reshape(length, 3, head_count, head_width)
    queries = head_norm(split_parts[:, 0].astype(jnp.float32), query_gain).astype(jnp.bfloat16)
    key_rows = head_norm(split_parts[:, 1].astype(jnp.float32), key_gain).astype(jnp.bfloat16)
    scores = jnp.einsum(
        "qhd,khd->hqk", queries, key_rows, preferred_element_type=jnp.float32
    ) / math.sqrt(head_width)
    same_image = seg_rows[:, None] == seg_rows[None, :]
    raised = jnp.where(same_image[None], jnp.exp(scores), 0.0)
    weights = (raised / jnp.sum(raised, axis=-1, keepdims=True)).astype(jnp.bfloat16)
    head_out = jnp.einsum(
        "hqk,khd->qhd", weights, split_parts[:, 2], preferred_element_type=jnp.float32
    )
    return head_out.reshape(length, head_count * head_width).astype(jnp.bfloat16)


def project_home(heads_local, resid_rows, out_weight):
    gathered = lax.all_gather(heads_local, "mp", axis=1, tiled=True)
    running = resid_rows.astype(jnp.float32) + jnp.dot(
        gathered,
        lax.all_gather(out_weight, "dp", axis=0, tiled=True),
        preferred_element_type=jnp.float32,
    )
    return running.astype(jnp.bfloat16)


def pool(row_mixed, seg_rows, count_row):
    images = count_row.shape[0]
    member_ids = lax.broadcasted_iota(jnp.int32, (images, seg_rows.shape[0]), 0)
    member = (member_ids == seg_rows[None, :]).astype(jnp.bfloat16)
    image_sums = jnp.dot(member, row_mixed, preferred_element_type=jnp.float32)
    return (image_sums / count_row[:, None].astype(jnp.float32)).astype(jnp.bfloat16)


def label_terms(pooled, label_weight):
    return jnp.einsum(
        "abd,dc->abc",
        lax.all_gather(pooled[None], "dp", axis=0, tiled=True),
        label_weight,
        preferred_element_type=jnp.float32,
    )


def pick(values, row_index, is_valid):
    taken = jnp.take(values, row_index, axis=0)
    taken = taken.reshape(is_valid.shape + values.shape[1:])
    keep_mask = is_valid.reshape(is_valid.shape + (1,) * (values.ndim - 1))
    return jnp.where(keep_mask, taken, jnp.zeros_like(taken))


def on_device(
    qkv_home,
    resid_home,
    out_weight,
    label_weight,
    label_bias,
    query_gain,
    key_gain,
    patch_counts,
    move_plan,
    segment_ids,
):
    row_count = lax.axis_size("dp")
    my_index = lax.axis_index("dp")
    home_slots = segment_ids.shape[1]
    pair_slots = home_slots // row_count
    image_ids = lax.broadcasted_iota(jnp.int32, (row_count, row_count, row_count), 2)
    image_ends = jnp.cumsum(patch_counts, axis=1)
    starts = image_ends - patch_counts
    matches = (move_plan[:, :, None] == image_ids).astype(jnp.int32)
    image_sizes = jnp.sum(patch_counts[:, :, None] * matches, axis=1)
    firsts = jnp.sum(starts[:, :, None] * matches, axis=1)
    send_sizes = lax.dynamic_index_in_dim(image_sizes, my_index, 0, keepdims=False)
    send_firsts = lax.dynamic_index_in_dim(firsts, my_index, 0, keepdims=False)
    within = lax.broadcasted_iota(jnp.int32, (row_count, pair_slots), 1)
    send_valid = within < send_sizes[:, None]
    send_index = jnp.minimum(send_firsts[:, None] + within, home_slots - 1).reshape(-1)
    arrive_sizes = lax.dynamic_index_in_dim(image_sizes, my_index, 1, keepdims=False)
    arrive_ends = jnp.cumsum(arrive_sizes)
    arrive_starts = arrive_ends - arrive_sizes
    slot_grid = lax.broadcasted_iota(jnp.int32, (TOK, row_count), 0)
    source = jnp.sum((slot_grid >= arrive_ends[None, :]).astype(jnp.int32), axis=1)
    chosen = (source[:, None] == lax.broadcasted_iota(jnp.int32, (TOK, row_count), 1)).astype(
        jnp.int32
    )
    arrive_index = (
        source * pair_slots + slot_grid[:, 0] - jnp.sum(chosen * arrive_starts[None, :], axis=1)
    )
    home_mixed = project_home(
        attend_home(qkv_home[0], segment_ids[0], query_gain, key_gain), resid_home[0], out_weight
    )
    count_row = lax.dynamic_index_in_dim(patch_counts, my_index, 0, keepdims=False)
    pooled = pool(home_mixed, segment_ids[0], count_row)
    partial_value = label_terms(pooled, label_weight)
    send_mixed = pick(home_mixed, send_index, send_valid)
    got_mixed = lax.all_to_all(send_mixed, "dp", split_axis=0, concat_axis=0, tiled=True)
    mixed = jnp.take(got_mixed.reshape(row_count * pair_slots, -1), arrive_index, axis=0)
    logit_sums = lax.psum_scatter(
        partial_value.astype(jnp.bfloat16), "mp", scatter_dimension=1, tiled=True
    ).astype(jnp.float32)
    class_probs = jax.nn.sigmoid(logit_sums + label_bias[None, None, :])
    labels = lax.all_to_all(
        class_probs.astype(jnp.bfloat16), "dp", split_axis=0, concat_axis=2, tiled=True
    ).astype(class_probs.dtype)
    return (mixed[None], labels)

def solution(mesh):
    rows, parts, sharers = (mesh.shape[name] for name in ("dp", "mp", "groups"))
    small = rows == parts == 4 and sharers == 2
    return jax.shard_map(
        on_device_rings if small else on_device,
        mesh=mesh,
        in_specs=(
            P(("groups", "dp"), None, None, "mp"),
            P(("groups", "dp"), None, "mp"),
            P("dp", "mp"),
            P("mp", "dp"),
            P("dp"),
            P(),
            P(),
            P("groups", None),
            P("groups", None),
            P(("groups", "dp"), None),
        ),
        out_specs=(P(("groups", "dp"), None, "mp"), P(("groups", "dp"), "mp", None)),
        check_vma=False,
    )
```

```python
import math

import jax
import jax.numpy as jnp
from jax import lax
from jax.experimental import pallas as pl
from jax.experimental.pallas import tpu as pltpu
from jax.sharding import PartitionSpec as P

TOK = 384
CHUNKS = 2
VMEM_BYTES = 24 * 1024 * 1024
EARLY_FLOPS = 4_000_000_000


EPSILON = 1e-06


def head_norm(values, norm_gain):
    center = values - jnp.mean(values, axis=-1, keepdims=True)
    spread = jnp.mean(center * center, axis=-1, keepdims=True)
    return center * lax.rsqrt(spread + EPSILON) * norm_gain


def shifted(count, by):
    return [(i, (i + by) % count) for i in range(count)]


def crossed(count, by):
    return [(i, i ^ by) for i in range(count)]


def send(values, axis, pairs, name):
    with jax.named_scope(name):
        return lax.ppermute(values, axis, pairs)


def dot32(left, right):
    return jnp.dot(left, right, preferred_element_type=jnp.float32)


def at(values, index, axis=0):
    return lax.dynamic_index_in_dim(values, index, axis, keepdims=False)


def image_for(counts_ref, plan_ref, row, dest, images):
    image, first, size, before = 0, 0, 0, 0
    for j in range(images):
        count = counts_ref[row, j]
        hit = plan_ref[row, j] == dest
        image = jnp.where(hit, j, image)
        first = jnp.where(hit, before, first)
        size = jnp.where(hit, count, size)
        before = before + count
    return image, first, size


def attend_kernel(
    rows,
    span,
    place_ref,
    counts_ref,
    plan_ref,
    qkv_ref,
    resid_ref,
    query_gain_ref,
    key_gain_ref,
    *rest,
):
    heads_ref, sent_ref, resid_means_ref, means_ref = rest[-4:]
    k = pl.program_id(0)
    lines = pl.ds(pl.multiple_of(k * span, 16), span)
    my_row = place_ref[0]
    image, first, size = image_for(
        counts_ref, plan_ref, my_row, lax.rem(my_row + k, rows), rows
    )
    window = span + 16
    begin = pl.multiple_of(first // 16 * 16, 16)
    shift = first - begin
    taken = lax.broadcasted_iota(jnp.int32, (span, window), 0)
    slot = lax.broadcasted_iota(jnp.int32, (span, window), 1)
    select = ((slot - taken == shift) & (taken < size)).astype(jnp.float32).astype(jnp.bfloat16)
    count = size.astype(jnp.float32)
    resid = dot32(select, resid_ref[pl.ds(begin, window), :])
    sent_ref[...] = resid.astype(jnp.bfloat16)
    here = lax.broadcasted_iota(jnp.int32, (means_ref.shape[0], 1), 0) == image
    resid_mean = jnp.sum(resid, axis=0, keepdims=True) / count
    resid_means_ref[...] = jnp.where(here, resid_mean, resid_means_ref[...])

    @pl.when(k == 0)
    def _():
        means_ref[...] = jnp.zeros_like(means_ref)
    queries = dot32(select, qkv_ref[0, pl.ds(begin, window), :])
    keys = dot32(select, qkv_ref[1, pl.ds(begin, window), :])
    values = dot32(select, qkv_ref[2, pl.ds(begin, window), :]).astype(jnp.bfloat16)
    head_width = query_gain_ref.shape[1]
    inside = lax.broadcasted_iota(jnp.int32, (span, span), 1) < size
    kept = lax.broadcasted_iota(jnp.int32, (span, 1), 0) < size
    for h in range(heads_ref.shape[1] // head_width):
        columns = slice(h * head_width, (h + 1) * head_width)
        query = head_norm(queries[:, columns], query_gain_ref[...]).astype(jnp.bfloat16)
        key = head_norm(keys[:, columns], key_gain_ref[...]).astype(jnp.bfloat16)
        scores = lax.dot_general(
            query, key, (((1,), (1,)), ((), ())), preferred_element_type=jnp.float32
        ) * (1.0 / math.sqrt(head_width))
        raised = jnp.where(inside, jnp.exp(scores), 0.0)
        scale = jnp.where(kept, 1.0 / jnp.sum(raised, axis=-1, keepdims=True), 0.0)
        weights = (raised * scale).astype(jnp.bfloat16)
        head = dot32(weights, values[:, columns]).astype(jnp.bfloat16)
        heads_ref[lines, columns] = head
        head_mean = jnp.sum(head.astype(jnp.float32), axis=0, keepdims=True) / count
        means_ref[:, columns] = jnp.where(here, head_mean, means_ref[:, columns])

    @pl.when(k == rows - 1)
    def _():
        heads_ref[rows * span :, :] = means_ref[...].astype(jnp.bfloat16)


def attend(place, counts, plan, qkv, resid, query_gain, key_gain, span, after):
    rows = counts.shape[0]
    local, features = qkv.shape[2], resid.shape[1]
    extra = -(-rows // 16) * 16
    fixed = lambda shape: pl.BlockSpec(shape, lambda k, *_: (0,) * len(shape))
    return pl.pallas_call(
        lambda *refs: attend_kernel(rows, span, *refs),
        grid_spec=pltpu.PrefetchScalarGridSpec(
            num_scalar_prefetch=3,
            grid=(rows,),
            in_specs=[fixed(x.shape) for x in (qkv, resid, query_gain, key_gain)]
            + [pl.BlockSpec(memory_space=pl.ANY)] * len(after),
            out_specs=[
                fixed((rows * span + extra, local)),
                pl.BlockSpec((span, features), lambda k, *_: (k, 0)),
                fixed((extra, features)),
            ],
            scratch_shapes=[pltpu.VMEM((extra, local), jnp.float32)],
        ),
        out_shape=[
            jax.ShapeDtypeStruct((rows * span + extra, local), jnp.bfloat16),
            jax.ShapeDtypeStruct((rows * span, features), jnp.bfloat16),
            jax.ShapeDtypeStruct((extra, features), jnp.float32),
        ],
        compiler_params=pltpu.CompilerParams(vmem_limit_bytes=VMEM_BYTES),
        cost_estimate=pl.CostEstimate(
            flops=10_000_000_000, bytes_accessed=12_000_000, transcendentals=0
        ),
        name="attend",
    )(place, counts, plan, qkv, resid, query_gain, key_gain, *after)


def early_kernel(rows, with_late, place_ref, *refs):
    head_refs = refs[:rows]
    own_ref, *piece_refs = refs[rows : rows + 4]
    resid_ref, means_ref = refs[rows + 4 : rows + 6]
    held_ref, weight_ref, head_sems, weight_sems, late_sem = refs[-5:]
    total_ref, late_ref = refs[-7:-5] if with_late else (refs[-6], None)
    my_row, my_part, my_group = place_ref[0], place_ref[1], place_ref[2]
    tiles, used, tile = weight_ref.shape
    depth = head_refs[0].shape[1]
    half = depth // 2

    def head_copies(act):
        for x in range(rows):
            step = lax.rem(my_row - (x ^ my_part) + rows, rows)
            for s in range(2):
                turned = jnp.where(step == 0, s, s ^ my_group)
                start = pl.multiple_of(step * depth + turned * half, 128)
                copy = pltpu.make_async_copy(
                    head_refs[x].at[: held_ref.shape[0], s * half : (s + 1) * half],
                    held_ref.at[:, pl.ds(start, half)],
                    head_sems.at[x, s],
                )
                act(copy)

    def weight_copies(i, act):
        column = i * tile
        sources = [own_ref.at[:, column : column + tile]]
        sources += [piece_ref.at[:, column : column + tile] for piece_ref in piece_refs]
        starts = [0, depth, depth + half, depth + 2 * half]
        for n, (source, start) in enumerate(zip(sources, starts)):
            act(
                pltpu.make_async_copy(
                    source, weight_ref.at[i, pl.ds(start, source.shape[0])], weight_sems.at[i, n]
                )
            )

    i = pl.program_id(0)

    @pl.when(i == 0)
    def _():
        head_copies(lambda copy: copy.start())
        for j in range(tiles):
            weight_copies(j, lambda copy: copy.start())
        head_copies(lambda copy: copy.wait())
        if with_late:
            pltpu.make_async_copy(held_ref.at[:, used:], late_ref, late_sem).start()

    for j in range(tiles):

        @pl.when(i == j)
        def _():
            weight_copies(j, lambda copy: copy.wait())

    length = resid_ref.shape[0]
    for start in range(0, length, 256):
        added = min(256, length - start)
        last = start + added == length
        lines = slice(start, None if last else start + added)
        total = dot32(held_ref[lines, :used], weight_ref[i])
        lines = slice(start, start + added)
        total_ref[lines] = total[:added] + resid_ref[lines].astype(jnp.float32)
        if last:
            total_ref[length:] = total[added:] + means_ref[...]

    if with_late:

        @pl.when(i == tiles - 1)
        def _():
            pltpu.make_async_copy(held_ref.at[:, used:], late_ref, late_sem).wait()


def project_early(place, heads, own, pieces, resid, means, chunk, with_late, after):
    rows = len(heads)
    length, depth = heads[0].shape
    width = pieces[0].shape[1]
    used = depth * 5 // 2
    tile = 256
    tiles = width // tile
    anywhere = pl.BlockSpec(memory_space=pl.ANY)
    late = [jax.ShapeDtypeStruct((length, rows * depth - used), jnp.bfloat16)] if with_late else []
    return pl.pallas_call(
        lambda place_ref, *refs: early_kernel(
            rows, with_late, place_ref, *refs[: rows + 6], *refs[rows + 6 + len(after) :]
        ),
        grid=(tiles,),
        in_specs=[pl.BlockSpec(memory_space=pltpu.SMEM)]
        + [anywhere] * (rows + 4)
        + [
            pl.BlockSpec((x.shape[0], tile), lambda i: (0, chunk * tiles + i))
            for x in (resid, means)
        ]
        + [anywhere] * len(after),
        out_specs=[pl.BlockSpec((length, tile), lambda i: (0, i))] + [anywhere] * len(late),
        scratch_shapes=[
            pltpu.VMEM((length, rows * depth), jnp.bfloat16),
            pltpu.VMEM((tiles, used, tile), jnp.bfloat16),
            pltpu.SemaphoreType.DMA((rows, 2)),
            pltpu.SemaphoreType.DMA((tiles, 4)),
            pltpu.SemaphoreType.DMA,
        ],
        out_shape=[jax.ShapeDtypeStruct((length, width), jnp.float32)] + late,
        compiler_params=pltpu.CompilerParams(vmem_limit_bytes=VMEM_BYTES),
        cost_estimate=pl.CostEstimate(
            flops=EARLY_FLOPS, bytes_accessed=1000, transcendentals=0
        ),
        name="project_early",
    )(place, *heads, own, *pieces, resid, means, *after)


def late_kernel(rows, total_ref, late_ref, *refs):
    piece_refs, out_refs = refs[:3], refs[-rows:]
    span = out_refs[0].shape[0]
    weights = jnp.concatenate([piece_ref[...] for piece_ref in piece_refs], axis=0)
    for k in range(rows):
        lines = slice(k * span, (k + 1) * span)
        total = total_ref[lines, :] + dot32(late_ref[lines, :], weights)
        out_refs[k][...] = total.astype(jnp.bfloat16)


def pool_kernel(rows, chunks, *refs):
    late_ref, total_refs = refs[0], refs[1 : 1 + chunks]
    piece_refs, pooled_ref = refs[1 + chunks : -1], refs[-1]
    half, width = piece_refs[0].shape
    for c in range(chunks):
        total = total_refs[c][...]
        for n in range(3):
            columns = slice(n * half, (n + 1) * half)
            total = total + dot32(late_ref[:, columns], piece_refs[3 * c + n][...])
        pooled_ref[:, c * width : (c + 1) * width] = total[:rows].astype(jnp.bfloat16)


def project_pooled(totals, late, pieces, rows, start):
    chunks = len(totals)
    extra = late.shape[0] - start
    width = totals[0].shape[1]
    flat = [piece for chunk in pieces for piece in chunk]
    whole = lambda x: pl.BlockSpec(x.shape, lambda i: (0, 0))
    tail = lambda x: pl.BlockSpec((extra, x.shape[1]), lambda i: (start // extra, 0))
    return pl.pallas_call(
        lambda *refs: pool_kernel(rows, chunks, *refs),
        grid=(1,),
        in_specs=[tail(late)] + [tail(x) for x in totals] + [whole(x) for x in flat],
        out_specs=pl.BlockSpec((rows, chunks * width), lambda i: (0, 0)),
        out_shape=jax.ShapeDtypeStruct((rows, chunks * width), jnp.bfloat16),
        compiler_params=pltpu.CompilerParams(vmem_limit_bytes=VMEM_BYTES),
        cost_estimate=pl.CostEstimate(flops=1000, bytes_accessed=1000, transcendentals=0),
        name="project_pooled",
    )(late, *totals, *flat)


def project_late(total, late, pieces, rows, span, after):
    half, width = pieces[0].shape
    length = total.shape[0]
    tile = 256
    tiles = width // tile
    return pl.pallas_call(
        lambda *refs: late_kernel(rows, *refs),
        grid=(tiles,),
        in_specs=[
            pl.BlockSpec((length, tile), lambda i: (0, i)),
            pl.BlockSpec(late.shape, lambda i: (0, 0)),
        ]
        + [pl.BlockSpec((half, tile), lambda i: (0, i))] * 3
        + [pl.BlockSpec(memory_space=pl.ANY)] * len(after),
        out_specs=[pl.BlockSpec((span, tile), lambda i: (0, i))] * rows,
        out_shape=[jax.ShapeDtypeStruct((span, width), jnp.bfloat16)] * rows,
        compiler_params=pltpu.CompilerParams(vmem_limit_bytes=VMEM_BYTES),
        cost_estimate=pl.CostEstimate(
            flops=6 * length * half * width, bytes_accessed=6_000_000, transcendentals=0
        ),
        name="project_late",
    )(total, late, *pieces, *after)


def one_hot(hits):
    return hits.astype(jnp.float32).astype(jnp.bfloat16)


def local_call(kernel, out_shape, operands, after, place, name, flops):
    whole = pl.BlockSpec(memory_space=pltpu.VMEM)
    return pl.pallas_call(
        kernel,
        in_specs=[pl.BlockSpec(memory_space=pltpu.SMEM)]
        + [whole] * len(operands)
        + [pl.BlockSpec(memory_space=pl.ANY)] * len(after),
        out_specs=jax.tree.map(lambda _: whole, out_shape),
        out_shape=out_shape,
        compiler_params=pltpu.CompilerParams(vmem_limit_bytes=VMEM_BYTES),
        cost_estimate=pl.CostEstimate(flops=flops, bytes_accessed=1000, transcendentals=0),
        name=name,
    )(place, *operands, *after)


def after_all(values, after):
    return lax.optimization_barrier((list(values), list(after)))[0]


def terms_kernel(rows, place_ref, *refs):
    pooled_refs = refs[:rows]
    weight_ref = refs[rows]
    out_refs = refs[-rows - 1 : -1]
    pooled_ref = refs[-1]
    count = rows * rows

    @pl.when(pl.program_id(0) == 0)
    def _():
        wanted = lax.broadcasted_iota(jnp.int32, (count, rows), 0)
        image = lax.broadcasted_iota(jnp.int32, (count, rows), 1)
        part = wanted // rows ^ place_ref[1]
        pooled = None
        for k in range(rows):
            row = lax.rem(place_ref[0] - k + rows, rows)
            order = one_hot((wanted % rows == row) & (image == part))
            term = dot32(order, pooled_refs[k][...])
            pooled = term if pooled is None else pooled + term
        pooled_ref[...] = pooled.astype(jnp.bfloat16)

    terms = dot32(pooled_ref[...], weight_ref[...]).astype(jnp.bfloat16)
    for k in range(rows):
        out_refs[k][...] = terms[k * rows : (k + 1) * rows]


def label_terms_by_part(place, pooled, label_weight, after):
    rows = len(pooled)
    features, classes = label_weight.shape
    tile = 512
    return pl.pallas_call(
        lambda *refs: terms_kernel(rows, *refs),
        grid_spec=pltpu.PrefetchScalarGridSpec(
            num_scalar_prefetch=1,
            grid=(classes // tile,),
            in_specs=[pl.BlockSpec(x.shape, lambda i, *_: (0, 0)) for x in pooled]
            + [pl.BlockSpec((features, tile), lambda i, *_: (0, i))]
            + [pl.BlockSpec(memory_space=pl.ANY)] * len(after),
            out_specs=[pl.BlockSpec((rows, tile), lambda i, *_: (0, i))] * rows,
            scratch_shapes=[pltpu.VMEM((rows * rows, features), jnp.bfloat16)],
        ),
        out_shape=[jax.ShapeDtypeStruct((rows, classes), jnp.bfloat16)] * rows,
        compiler_params=pltpu.CompilerParams(vmem_limit_bytes=VMEM_BYTES),
        cost_estimate=pl.CostEstimate(
            flops=2 * rows * rows * features * classes,
            bytes_accessed=12_000_000,
            transcendentals=0,
        ),
        name="label_terms",
    )(place, *pooled, label_weight, *after)


def probs_kernel(rows, place_ref, *refs):
    term_refs = refs[:rows]
    bias_ref = refs[rows]
    out_refs = refs[-rows:]
    logits = term_refs[0][...].astype(jnp.float32)
    for k in range(1, rows):
        logits = logits + term_refs[k][...].astype(jnp.float32)
    probs = jax.nn.sigmoid(logits + bias_ref[...])
    line = lax.broadcasted_iota(jnp.int32, (rows, 1), 0)
    for k in range(rows):
        row = lax.rem(place_ref[0] + k, rows)
        picked = jnp.sum(jnp.where(line == row, probs, 0.0), axis=0, keepdims=True)
        out_refs[k][...] = picked.astype(jnp.bfloat16)


def labels_kernel(rows, place_ref, *refs):
    out_ref = refs[-1]
    classes = refs[0].shape[1]
    for k in range(rows):
        row = lax.rem(place_ref[0] - k + rows, rows)
        columns = pl.ds(pl.multiple_of(row * classes, 128), classes)
        out_ref[:, columns] = refs[k][...].astype(jnp.float32)


def settle_kernel(rows, place_ref, counts_ref, plan_ref, *refs):
    block_refs = refs[:rows]
    out_ref = refs[-1]
    my_row = place_ref[0]
    tokens, span = out_ref.shape[0], block_refs[0].shape[0]
    token = lax.broadcasted_iota(jnp.int32, (tokens, span), 0)
    slot = lax.broadcasted_iota(jnp.int32, (tokens, span), 1)
    sizes = [image_for(counts_ref, plan_ref, r, my_row, rows)[2] for r in range(rows)]
    total = None
    for k in range(rows):
        source = lax.rem(my_row - k + rows, rows)
        start, size = 0, 0
        for r in range(rows):
            start = start + jnp.where(r < source, sizes[r], 0)
            size = jnp.where(r == source, sizes[r], size)
        select = ((token - slot == start) & (slot < size)).astype(jnp.float32).astype(jnp.bfloat16)
        term = dot32(select, block_refs[k][...])
        total = term if total is None else total + term
    out_ref[...] = total.astype(jnp.bfloat16)


def settle(place, counts, plan, blocks, chunk, features, earlier, after):
    rows = len(blocks)
    span, width = blocks[0].shape
    tile = 256
    tiles = width // tile
    first = chunk * tiles
    more = [] if earlier is None else [earlier]
    return pl.pallas_call(
        lambda *refs: settle_kernel(rows, *refs),
        grid_spec=pltpu.PrefetchScalarGridSpec(
            num_scalar_prefetch=3,
            grid=(tiles,),
            in_specs=[pl.BlockSpec((span, tile), lambda i, *_: (0, i))] * rows
            + [pl.BlockSpec(memory_space=pl.ANY)] * (len(more) + len(after)),
            out_specs=pl.BlockSpec((TOK, tile), lambda i, *_: (0, first + i)),
        ),
        out_shape=jax.ShapeDtypeStruct((TOK, features), jnp.bfloat16),
        input_output_aliases={3 + rows: 0} if more else {},
        compiler_params=pltpu.CompilerParams(vmem_limit_bytes=VMEM_BYTES),
        cost_estimate=pl.CostEstimate(
            flops=2 * TOK * rows * span * width, bytes_accessed=2_000_000, transcendentals=0
        ),
        name="settle",
    )(place, counts, plan, *blocks, *more, *after)


def on_device_rings(
    qkv_home,
    resid_home,
    out_weight,
    label_weight,
    label_bias,
    query_gain,
    key_gain,
    patch_counts,
    move_plan,
    segment_ids,
):
    rows = lax.axis_size("dp")
    parts = lax.axis_size("mp")
    sharers = lax.axis_size("groups")
    my_row = lax.axis_index("dp")
    my_part = lax.axis_index("mp")
    my_group = lax.axis_index("groups")
    slots = segment_ids.shape[1]
    span = -(-(slots // rows) // 16) * 16
    padded = -(-slots // 16) * 16 + span
    depth, features = out_weight.shape
    half = depth // sharers
    width = features // CHUNKS
    place = jnp.stack([my_row, my_part, my_group]).astype(jnp.int32)

    mine = lax.dynamic_slice_in_dim(out_weight, my_group * half, half, 0)
    moving = [mine[:, c * width : (c + 1) * width] for c in range(CHUNKS)]
    moving = [send(x, "dp", shifted(rows, 1), f"w{c}_1") for c, x in enumerate(moving)]

    qkv = jnp.pad(jnp.transpose(qkv_home[0], (1, 0, 2)), ((0, 0), (0, padded - slots), (0, 0)))
    heads, resid, resid_means = attend(
        place,
        patch_counts,
        move_plan,
        qkv,
        jnp.pad(resid_home[0], ((0, padded - slots), (0, 0))),
        query_gain[None],
        key_gain[None],
        span,
        [],
    )
    heads = after_all([heads], moving)[0]
    across = send(heads, "mp", crossed(parts, 2), "h_2")
    beside = send(heads, "mp", crossed(parts, 1), "h_1")

    following = [send(x, "dp", shifted(rows, 1), f"w{c}_2") for c, x in enumerate(moving)]
    others = [
        send(x, "groups", crossed(sharers, 1), f"y{c}_1") for c, x in enumerate(moving)
    ]
    pieces = [[x, y, z] for x, y, z in zip(moving, others, following)]
    turned = after_all([across], [*following, *others])[0]
    beyond = send(turned, "mp", crossed(parts, 1), "h_3")
    every_head = [heads, beside, across, beyond]

    totals, late, early, moving = [], None, pieces, following
    pieces = []
    for c in range(CHUNKS):
        after = totals
        x = after_all([moving[c]], after)[0] if c else moving[c]
        x = send(x, "dp", shifted(rows, 1), f"w{c}_3")
        total, *more = project_early(
            place,
            every_head,
            out_weight[:, c * width : (c + 1) * width],
            early[c],
            resid,
            resid_means,
            c,
            c == 0,
            [totals[0], pieces[0][1]] if c else [],
        )
        totals.append(total)
        late = more[0] if more else late
        y = after_all([moving[c]], [x, total, pieces[0][2]])[0] if c else moving[c]
        y = send(y, "groups", crossed(sharers, 1), f"y{c}_2")
        z = after_all([x], [total] if c else [total, y])[0]
        z = send(z, "groups", crossed(sharers, 1), f"y{c}_3")
        pieces.append([y, x, z])

    arrived = []
    for c in range(CHUNKS):
        if c == CHUNKS - 1:
            pooled = project_pooled(totals, late, pieces, rows, rows * span)
            pooled = [pooled] + [
                send(pooled, "dp", shifted(rows, k), f"p_{k}") for k in range(1, rows)
            ]
        blocks = project_late(
            totals[c], late, pieces[c], rows, span, arrived[0][1:] if c else []
        )
        if c == CHUNKS - 1:
            blocks = after_all(blocks, pooled[1:])
        arrived.append(
            [blocks[0]] + [send(blocks[k], "dp", shifted(rows, k), f"m{c}_{k}") for k in range(1, rows)]
        )

    classes = label_weight.shape[1]
    terms = label_terms_by_part(place, pooled, label_weight, [])
    terms = [terms[0]] + [
        send(terms[k], "mp", crossed(parts, k), f"t_{k}") for k in range(1, parts)
    ]
    probs = local_call(
        lambda *refs: probs_kernel(rows, *refs),
        [jax.ShapeDtypeStruct((1, classes), jnp.bfloat16)] * rows,
        [*terms, label_bias[None]],
        [],
        place,
        "probs",
        1000,
    )
    probs = [probs[0]] + [send(probs[k], "dp", shifted(rows, k), f"l_{k}") for k in range(1, rows)]
    mixed = None
    for c in range(CHUNKS):
        mixed = settle(place, patch_counts, move_plan, arrived[c], c, features, mixed, [])
    labels = local_call(
        lambda *refs: labels_kernel(rows, *refs),
        jax.ShapeDtypeStruct((1, rows * classes), jnp.float32),
        after_all(probs, [mixed]),
        [],
        place,
        "labels",
        1000,
    )
    labels = labels[None]
    return (mixed[None], labels)

def attend_home(qkv_rows, seg_rows, query_gain, key_gain):
    length = qkv_rows.shape[0]
    head_width = query_gain.shape[0]
    head_count = qkv_rows.shape[2] // head_width
    split_parts = qkv_rows.reshape(length, 3, head_count, head_width)
    queries = head_norm(split_parts[:, 0].astype(jnp.float32), query_gain).astype(jnp.bfloat16)
    key_rows = head_norm(split_parts[:, 1].astype(jnp.float32), key_gain).astype(jnp.bfloat16)
    scores = jnp.einsum(
        "qhd,khd->hqk", queries, key_rows, preferred_element_type=jnp.float32
    ) / math.sqrt(head_width)
    same_image = seg_rows[:, None] == seg_rows[None, :]
    raised = jnp.where(same_image[None], jnp.exp(scores), 0.0)
    weights = (raised / jnp.sum(raised, axis=-1, keepdims=True)).astype(jnp.bfloat16)
    head_out = jnp.einsum(
        "hqk,khd->qhd", weights, split_parts[:, 2], preferred_element_type=jnp.float32
    )
    return head_out.reshape(length, head_count * head_width).astype(jnp.bfloat16)


def project_home(heads_local, resid_rows, out_weight):
    gathered = lax.all_gather(heads_local, "mp", axis=1, tiled=True)
    running = resid_rows.astype(jnp.float32) + jnp.dot(
        gathered,
        lax.all_gather(out_weight, "dp", axis=0, tiled=True),
        preferred_element_type=jnp.float32,
    )
    return running.astype(jnp.bfloat16)


def pool(row_mixed, seg_rows, count_row):
    images = count_row.shape[0]
    member_ids = lax.broadcasted_iota(jnp.int32, (images, seg_rows.shape[0]), 0)
    member = (member_ids == seg_rows[None, :]).astype(jnp.bfloat16)
    image_sums = jnp.dot(member, row_mixed, preferred_element_type=jnp.float32)
    return (image_sums / count_row[:, None].astype(jnp.float32)).astype(jnp.bfloat16)


def label_terms(pooled, label_weight):
    return jnp.einsum(
        "abd,dc->abc",
        lax.all_gather(pooled[None], "dp", axis=0, tiled=True),
        label_weight,
        preferred_element_type=jnp.float32,
    )


def pick(values, row_index, is_valid):
    taken = jnp.take(values, row_index, axis=0)
    taken = taken.reshape(is_valid.shape + values.shape[1:])
    keep_mask = is_valid.reshape(is_valid.shape + (1,) * (values.ndim - 1))
    return jnp.where(keep_mask, taken, jnp.zeros_like(taken))


def on_device(
    qkv_home,
    resid_home,
    out_weight,
    label_weight,
    label_bias,
    query_gain,
    key_gain,
    patch_counts,
    move_plan,
    segment_ids,
):
    row_count = lax.axis_size("dp")
    my_index = lax.axis_index("dp")
    home_slots = segment_ids.shape[1]
    pair_slots = home_slots // row_count
    image_ids = lax.broadcasted_iota(jnp.int32, (row_count, row_count, row_count), 2)
    image_ends = jnp.cumsum(patch_counts, axis=1)
    starts = image_ends - patch_counts
    matches = (move_plan[:, :, None] == image_ids).astype(jnp.int32)
    image_sizes = jnp.sum(patch_counts[:, :, None] * matches, axis=1)
    firsts = jnp.sum(starts[:, :, None] * matches, axis=1)
    send_sizes = lax.dynamic_index_in_dim(image_sizes, my_index, 0, keepdims=False)
    send_firsts = lax.dynamic_index_in_dim(firsts, my_index, 0, keepdims=False)
    within = lax.broadcasted_iota(jnp.int32, (row_count, pair_slots), 1)
    send_valid = within < send_sizes[:, None]
    send_index = jnp.minimum(send_firsts[:, None] + within, home_slots - 1).reshape(-1)
    arrive_sizes = lax.dynamic_index_in_dim(image_sizes, my_index, 1, keepdims=False)
    arrive_ends = jnp.cumsum(arrive_sizes)
    arrive_starts = arrive_ends - arrive_sizes
    slot_grid = lax.broadcasted_iota(jnp.int32, (TOK, row_count), 0)
    source = jnp.sum((slot_grid >= arrive_ends[None, :]).astype(jnp.int32), axis=1)
    chosen = (source[:, None] == lax.broadcasted_iota(jnp.int32, (TOK, row_count), 1)).astype(
        jnp.int32
    )
    arrive_index = (
        source * pair_slots + slot_grid[:, 0] - jnp.sum(chosen * arrive_starts[None, :], axis=1)
    )
    home_mixed = project_home(
        attend_home(qkv_home[0], segment_ids[0], query_gain, key_gain), resid_home[0], out_weight
    )
    count_row = lax.dynamic_index_in_dim(patch_counts, my_index, 0, keepdims=False)
    pooled = pool(home_mixed, segment_ids[0], count_row)
    partial_value = label_terms(pooled, label_weight)
    send_mixed = pick(home_mixed, send_index, send_valid)
    got_mixed = lax.all_to_all(send_mixed, "dp", split_axis=0, concat_axis=0, tiled=True)
    mixed = jnp.take(got_mixed.reshape(row_count * pair_slots, -1), arrive_index, axis=0)
    logit_sums = lax.psum_scatter(
        partial_value.astype(jnp.bfloat16), "mp", scatter_dimension=1, tiled=True
    ).astype(jnp.float32)
    class_probs = jax.nn.sigmoid(logit_sums + label_bias[None, None, :])
    labels = lax.all_to_all(
        class_probs.astype(jnp.bfloat16), "dp", split_axis=0, concat_axis=2, tiled=True
    ).astype(class_probs.dtype)
    return (mixed[None], labels)

def solution(mesh):
    rows, parts, sharers = (mesh.shape[name] for name in ("dp", "mp", "groups"))
    small = rows == parts == 4 and sharers == 2
    return jax.shard_map(
        on_device_rings if small else on_device,
        mesh=mesh,
        in_specs=(
            P(("groups", "dp"), None, None, "mp"),
            P(("groups", "dp"), None, "mp"),
            P("dp", "mp"),
            P("mp", "dp"),
            P("dp"),
            P(),
            P(),
            P("groups", None),
            P("groups", None),
            P(("groups", "dp"), None),
        ),
        out_specs=(P(("groups", "dp"), None, "mp"), P(("groups", "dp"), "mp", None)),
        check_vma=False,
    )
```
